128 devices in a mesh: group: 2 (over x_lo), fsdp: 16 (over y, x_hi, core), seq: 4 (over z).
Axes of the slice: x: 4 (x_hi: 2, x_lo: 2; x = x_hi * 2 + x_lo), y: 4, z: 4, core: 2. Of those that a mesh axis runs over, the one named last changes fastest.
Arguments:
- latent_in: bfloat16 [16, 768, 3072], P('fsdp', 'seq'), may hold values from -6 to 6
- noise: bfloat16 [16, 768, 3072], P('fsdp', 'seq'), may hold values from -6 to 6
- timestep: int32 [16], P('fsdp'), may hold values from 0 to 999
- gen_gain: float32 [3072], replicated, may hold values from 0.25 to 1.75
- gen_qkv: bfloat16 [3072, 16, 3, 128], P('fsdp', ('group', 'seq')), may hold values from -0.109375 to 0.109375
- gen_out: bfloat16 [3072, 16, 128], P('fsdp', ('group', 'seq')), may hold values from -4 to 4
- score_gain: float32 [2, 3072], P('group'), may hold values from 0.25 to 1.75
- score_qkv: bfloat16 [3072, 2, 16, 3, 128], P(None, 'group', 'seq'), may hold values from -0.109375 to 0.109375
- score_out: bfloat16 [3072, 2, 16, 128], P(None, 'group', 'seq'), may hold values from -4 to 4
Outputs:
- generated: bfloat16 [16, 768, 3072], P('fsdp', 'seq')
- gen_grad: float32 [3072, 16, 3, 128], P('fsdp', ('group', 'seq'))
The draws below stay inside these ranges and needn't reach their ends.
All inputs are finite; a program needn't handle non-finite values.
Results may differ from the reference program's by a relative error of at most 0.023.
Values may be sent and summed in bfloat16 or wider, within the bound.
No kernel may reach another device: no remote copies, remote signals or barrier semaphores. Data moves between devices by JAX's collectives and lax.ppermute only.
A program may use at most 128 MiB of HBM per device.

```python
import jax
import jax.numpy as jnp
from jax import lax

D = 3072
HEADS = 16
HEAD = 128
SEQ_LEN = 768
STEPS = 1000
IMAGES = 16
N_GROUP = 2
N_SEQ = 4


def touch_ends(entries, stream_key, low, top_value):
    longest = entries.shape.index(max(entries.shape))
    spots = []
    for shift in (0, 1):
        where = [jax.random.randint(jax.random.fold_in(stream_key, axis), (), 0, length) for axis, length in enumerate(entries.shape)]
        where[longest] = (where[longest] + shift) % entries.shape[longest]
        spots.append(tuple(where))
    return entries.at[spots[0]].set(low).at[spots[1]].set(top_value)


def levels(rng, dims, shards, low, high):
    factor_of = 1.0
    for axis_at, blocks in shards:
        heights = jax.random.uniform(jax.random.fold_in(jax.random.fold_in(rng, 6), axis_at), (blocks,), jnp.float32, low / len(shards), high / len(shards))
        factor_of = factor_of * jnp.repeat(jnp.exp(heights), dims[axis_at] // blocks).reshape((-1,) + (1,) * (len(dims) - 1 - axis_at))
    return factor_of


def normal_values(own_key, extent, width, most, split=(), held_as=jnp.bfloat16):
    values = jax.random.normal(own_key, extent, jnp.float32) * width
    if len(split) > 0:
        values = levels(own_key, extent, split, -0.22, 0.18) * values
    return jnp.clip(values, min=-most, max=most).astype(held_as)


def setup_inputs(seed: int = 0) -> dict:
    key_list = jax.random.split(jax.random.key(seed), 10)
    latent_in = normal_values(key_list[0], (IMAGES, SEQ_LEN, D), 1.0, 6.0, ((0, 16), (1, 4)))
    noise = normal_values(key_list[1], (IMAGES, SEQ_LEN, D), 1.0, 6.0, ((0, 16), (1, 4)))
    timestep = touch_ends(jax.random.randint(key_list[2], (IMAGES,), 0, STEPS), jax.random.fold_in(key_list[2], 1), 0, STEPS - 1).astype(jnp.int32)
    gen_gain = jnp.clip(1.0 + 0.15 * jax.random.normal(key_list[3], (D,), jnp.float32), 0.25, 1.75)
    gen_qkv = normal_values(key_list[4], (D, HEADS, 3, HEAD), D ** -0.5, 0.109375, ((0, 16), (1, 8)))
    gen_out = normal_values(key_list[5], (D, HEADS, HEAD), (max(1, HEADS * HEAD // SEQ_LEN)) ** -0.5, 4.0, ((0, 16), (1, 8)))
    score_gain = jnp.clip(1.0 + 0.15 * jax.random.normal(key_list[6], (2, D), jnp.float32), 0.25, 1.75)
    score_qkv = normal_values(key_list[7], (D, 2, HEADS, 3, HEAD), D ** -0.5, 0.109375, ((1, 2), (2, 4)))
    score_out = normal_values(key_list[8], (D, 2, HEADS, HEAD), (max(1, HEADS * HEAD // SEQ_LEN)) ** -0.5, 4.0, ((1, 2), (2, 4)))
    return {"latent_in": latent_in, "noise": noise, "timestep": timestep, "gen_gain": gen_gain, "gen_qkv": gen_qkv, "gen_out": gen_out, "score_gain": score_gain, "score_qkv": score_qkv, "score_out": score_out}


SHIFT_FACTOR = 3.0
EPSILON = 1e-06

def rounded(values):
    return lax.optimization_barrier(values.astype(jnp.bfloat16)).astype(jnp.float32)

def normalize(values, gain_vector):
    inverse_rms = lax.rsqrt(lax.optimization_barrier(jnp.mean(values * values, axis=-1, keepdims=True)) + EPSILON)
    return (values * inverse_rms * gain_vector).astype(jnp.bfloat16)

def attend(projected):
    head_width = projected.shape[-1]
    queries = projected[:, :, 0]
    queries = queries * lax.rsqrt(lax.optimization_barrier(jnp.mean(queries * queries, axis=-1, keepdims=True)) + EPSILON) * head_width ** (-0.5)
    key_rows = projected[:, :, 1]
    key_rows = key_rows * lax.rsqrt(lax.optimization_barrier(jnp.mean(key_rows * key_rows, axis=-1, keepdims=True)) + EPSILON)
    scores = jnp.einsum('qhc,khc->hqk', rounded(queries), rounded(key_rows))
    weights = jnp.exp(scores)
    totals = lax.optimization_barrier(jnp.sum(weights, axis=-1))
    mixed_heads = jnp.einsum('hqk,khc->qhc', rounded(weights), rounded(projected[:, :, 2]))
    return mixed_heads / jnp.transpose(totals)[:, :, None]

def head_sum(mixed_heads, out_weight, groups):
    token_count = mixed_heads.shape[0]
    block_heads = mixed_heads.shape[1] // groups
    combined = jnp.zeros((token_count, out_weight.shape[0]), jnp.float32)
    for block_index in range(groups):
        low_head = block_index * block_heads
        mixed_block = mixed_heads[:, low_head:low_head + block_heads].reshape(token_count, -1)
        weight_block = out_weight[:, low_head:low_head + block_heads].reshape(out_weight.shape[0], -1)
        partial_term = lax.dot_general(mixed_block, weight_block, (((1,), (1,)), ((), ())), preferred_element_type=jnp.float32)
        combined = combined + rounded(partial_term)
    return combined

def score_branch(noisy, gain_vector, qkv_weight, out_weight):
    normed = normalize(noisy, gain_vector)
    projected = jnp.dot(normed, qkv_weight.reshape(D, -1), preferred_element_type=jnp.float32)
    projected = projected.reshape(SEQ_LEN, HEADS, 3, HEAD)
    mixed_heads = attend(projected).astype(jnp.bfloat16)
    return head_sum(mixed_heads, out_weight, N_SEQ)

def reference(latent_in, noise, timestep, gen_gain, gen_qkv, gen_out, score_gain, score_qkv, score_out):
    fraction = (timestep.astype(jnp.float32) + 1.0) / STEPS
    noise_level = SHIFT_FACTOR * fraction / (1.0 + (SHIFT_FACTOR - 1.0) * fraction)
    gen_matrix = gen_qkv.reshape(D, -1)
    gen_out_matrix = gen_out.reshape(D, -1)

    def one_image(accumulated, inputs):
        latent_rows, noise_rows, level = inputs
        normed = normalize(latent_rows.astype(jnp.float32), gen_gain)
        projected = jnp.dot(normed, gen_matrix, preferred_element_type=jnp.float32)
        projected = projected.reshape(SEQ_LEN, HEADS, 3, HEAD)
        mixed_raw, pullback = jax.vjp(attend, projected)
        update = head_sum(mixed_raw.astype(jnp.bfloat16), gen_out, N_GROUP * N_SEQ)
        generated = (latent_rows.astype(jnp.float32) + update).astype(jnp.bfloat16)
        noisy = (1.0 - level) * generated.astype(jnp.float32) + level * noise_rows.astype(jnp.float32)
        real_term = score_branch(noisy, score_gain[0], score_qkv[:, 0], score_out[:, 0])
        fake_term = score_branch(noisy, score_gain[1], score_qkv[:, 1], score_out[:, 1])
        cotangent = (-level / IMAGES * (fake_term - real_term)).astype(jnp.bfloat16)
        dmixed = jnp.dot(cotangent, gen_out_matrix, preferred_element_type=jnp.float32)
        dprojected = pullback(rounded(dmixed).reshape(SEQ_LEN, HEADS, HEAD))[0]
        dprojected = dprojected.astype(jnp.bfloat16).reshape(SEQ_LEN, -1)
        grad_term = lax.dot_general(normed, dprojected, (((0,), (0,)), ((), ())), preferred_element_type=jnp.float32)
        return (accumulated + rounded(grad_term), generated)
    start_grad = jnp.zeros((D, HEADS * 3 * HEAD), jnp.float32)
    gen_grad, generated = lax.scan(one_image, start_grad, (latent_in, noise, noise_level))
    return (generated, gen_grad.reshape(D, HEADS, 3, HEAD))
```

```python
import jax
import jax.numpy as jnp
from jax import lax
from jax.experimental import pallas as pl
from jax.experimental.pallas import tpu as pltpu
from jax.sharding import PartitionSpec as P

STEPS = 1000
SHIFT_FACTOR = 3.0
EPSILON = 1e-06
LOG2_E = 1.4426950408889634
LN_2 = 0.6931471805599453
F32 = jnp.float32
BF16 = jnp.bfloat16
VMEM = pl.BlockSpec(memory_space=pltpu.VMEM)
SMEM = pl.BlockSpec(memory_space=pltpu.SMEM)
ANY = pl.BlockSpec(memory_space=pl.ANY)


def like(shape, dtype):
    return jax.ShapeDtypeStruct(shape, dtype)


def memory(mebibytes):
    return pltpu.CompilerParams(vmem_limit_bytes=mebibytes * 2**20)


def shift(axis, size, stride, step):
    length = lax.axis_size(axis)
    moves = []
    for i in range(length):
        place = (i // stride) % size
        moves.append((i, i + ((place + step) % size - place) * stride))
    return lambda piece: lax.ppermute(piece, axis, moves)


def seq_ring():
    size = lax.axis_size("seq")
    return shift("seq", size, 1, -1), shift("seq", size, 1, 1)


def y_ring():
    size = lax.axis_size("fsdp") // 4
    return shift("fsdp", size, 4, -1), shift("fsdp", size, 4, 1)


def swap_group(piece):
    return shift("group", 2, 1, 1)(piece)


def swap_core(piece):
    return shift("fsdp", 2, 1, 1)(piece)


def swap_half(piece):
    return shift("fsdp", 2, 2, 1)(piece)


def ring_gather(shard, ring):
    to_left, to_right = ring
    half = shard.shape[0] // 2
    right = to_left(shard)
    left = to_right(shard)
    return [shard, right, to_left(right[:half]), to_right(left[half:]), left]


def ring_sum(left_first, right_first, held_left, held_right, ring, beside=None):
    to_left, to_right = ring
    half = held_left.shape[0]
    from_right = to_left(left_first)
    from_left = to_right(right_first)
    if beside is not None:
        from_right, from_left, beside = lax.optimization_barrier((from_right, from_left, beside))
    from_right_last = to_left((held_left + from_right[:half].astype(F32)).astype(BF16))
    from_left_last = to_right((held_right + from_left[:half].astype(F32)).astype(BF16))
    sums = (from_left, from_right, from_right_last, from_left_last)
    return sums if beside is None else (sums, beside)


def ring_total(own, from_left, from_right, from_right_last, from_left_last):
    half = own.shape[0] // 2
    first = own[:half] + from_left[half:].astype(F32) + from_right_last.astype(F32)
    second = own[half:] + from_right[half:].astype(F32) + from_left_last.astype(F32)
    return jnp.concatenate([first, second])


def ordered(flag, own, other):
    first = jnp.where(flag == 0, own, other)
    second = jnp.where(flag == 0, other, own)
    return first, second


def core_rows(shards, core):
    keep, send = [], []
    for shard in shards:
        width = shard.shape[1] // 2
        low, high = shard[:, :width], shard[:, width:]
        keep.append(jnp.where(core == 0, low, high))
        send.append(jnp.where(core == 0, high, low))
    own = jnp.concatenate(keep, axis=1)
    other = swap_core(jnp.concatenate(send, axis=1))
    return jnp.concatenate(ordered(core, own, other))


def normalize_kernel(place_ref, values_ref, gain_ref, out_ref):
    blocks = 4
    width = values_ref.shape[1] // blocks
    values = values_ref[...].astype(F32)
    inverse_rms = lax.rsqrt(jnp.mean(values * values, axis=-1, keepdims=True) + EPSILON)
    for block in range(blocks):
        source = pl.multiple_of(lax.rem(place_ref[0] + block, blocks) * width, 128)
        part = values_ref[:, pl.ds(source, width)].astype(F32)
        out_ref[:, block * width : (block + 1) * width] = (
            part * inverse_rms * gain_ref[:, pl.ds(source, width)]
        ).astype(BF16)


def normalize_turned(values, gain_vector, places):
    return pl.pallas_call(
        normalize_kernel,
        out_shape=like(values.shape, BF16),
        in_specs=[SMEM, VMEM, VMEM],
        out_specs=VMEM,
        compiler_params=memory(16),
    )(places, values, gain_vector[None])


def unit_rows(values, scale):
    mean = jnp.mean(values * values, axis=-1, keepdims=True)
    return values * lax.rsqrt(mean + EPSILON) * scale


def dot(left, right, left_dim=1, right_dim=0):
    return lax.dot_general(
        left, right, (((left_dim,), (right_dim,)), ((), ())), preferred_element_type=F32
    )


def mix_head(query, key, value, store):
    tokens, width = query.shape
    unit_query = unit_rows(query, LOG2_E * width**-0.5).astype(BF16)
    turned_key = unit_rows(key, 1.0).T.astype(BF16)
    value = value.astype(BF16)
    span = tokens // 3
    for first in range(0, tokens, span):
        weights = jnp.exp2(dot(unit_query[first : first + span], turned_key))
        totals = jnp.sum(weights, axis=-1, keepdims=True)
        store(first, (dot(weights.astype(BF16), value) / totals).astype(BF16))


def gather_parts(parts, target, sems):
    copies = []
    row = 0
    for index, part in enumerate(parts):
        rows = part.shape[0]
        copies.append(
            pltpu.make_async_copy(part, target.at[pl.ds(row, rows)], sems.at[index])
        )
        row += rows
    for copy in copies:
        copy.start()
    return copies


def project_mix(full_ref, weight_ref, projected_ref, mixed_ref):
    width = mixed_ref.shape[1]
    projected_ref[...] = dot(full_ref[...], weight_ref[:, : 3 * width])

    def store(first, rows):
        mixed_ref[first : first + rows.shape[0], :] = rows

    mix_head(
        projected_ref[:, :width],
        projected_ref[:, width : 2 * width],
        projected_ref[:, 2 * width :],
        store,
    )


def first_head_kernel(*refs):
    parts, (weight_ref, full_ref, projected_ref, mixed_ref, sems) = refs[:-5], refs[-5:]
    for copy in gather_parts(parts, full_ref, sems):
        copy.wait()
    project_mix(full_ref, weight_ref, projected_ref, mixed_ref)


def head_outputs(tokens, weight):
    width = weight.shape[1] // 4
    return [like((tokens, 3 * width), F32), like((tokens, width), BF16)]


def first_head(parts, weight):
    tokens = sum(part.shape[0] for part in parts)
    return pl.pallas_call(
        first_head_kernel,
        out_shape=[like((tokens, weight.shape[0]), BF16)] + head_outputs(tokens, weight),
        in_specs=[ANY] * len(parts) + [VMEM],
        out_specs=[VMEM] * 3,
        scratch_shapes=[pltpu.SemaphoreType.DMA((len(parts),))],
        compiler_params=memory(60),
    )(*parts, weight)


def next_head(full, weight):
    return pl.pallas_call(
        project_mix,
        out_shape=head_outputs(full.shape[0], weight),
        in_specs=[VMEM] * 2,
        out_specs=[VMEM] * 2,
        compiler_params=memory(32),
    )(full, weight)


def columns_kernel(places, buffer, out, sems):
    rows = out.shape[0] // 4
    first = buffer.shape[1] - out.shape[1]
    copies = []
    for block in range(4):
        place = pl.multiple_of(lax.rem(places[0] + block, 4) * rows, rows)
        copies.append(
            pltpu.make_async_copy(
                buffer.at[pl.ds(block * rows, rows), pl.ds(first, out.shape[1])],
                out.at[pl.ds(place, rows)],
                sems.at[block],
            )
        )
    for copy in copies:
        copy.start()
    for copy in copies:
        copy.wait()


def out_columns_in_order(places, buffer, width):
    return pl.pallas_call(
        columns_kernel,
        out_shape=like((buffer.shape[0], width), BF16),
        in_specs=[SMEM, ANY],
        out_specs=VMEM,
        scratch_shapes=[pltpu.SemaphoreType.DMA((4,))],
        compiler_params=memory(16),
    )(places, buffer)


def update_kernel(
    places, a_own, b_own, a_other, b_other, own_buffer, own_heads, other_buffer, other_heads,
    own, left, right, held_left, held_right, matrix, sems
):
    width = a_own.shape[1]
    size = own.shape[1] // 4
    copies = []
    for side, (buffer, heads) in enumerate(
        ((own_buffer, own_heads), (other_buffer, other_heads))
    ):
        for block in range(4):
            first = pl.multiple_of((2 * block + places[1]) * size, size)
            rows = pl.ds(block * size, size)
            for index, source in enumerate(
                (buffer.at[pl.ds(first, size), pl.ds(3 * width, width)], heads.at[rows])
            ):
                target = matrix.at[rows, pl.ds((2 * side + index) * width, width)]
                copies.append(
                    pltpu.make_async_copy(source, target, sems.at[side, 2 * block + index])
                )
    for copy in copies:
        copy.start()
    for copy in copies:
        copy.wait()
    mixed = jnp.concatenate([a_own[...], b_own[...], a_other[...], b_other[...]], axis=1)
    rows = own.shape[0]
    half = rows // 2

    def term(first, count):
        return dot(mixed[first : first + count], matrix[...], 1, 1)

    two = term(2 * rows, rows)
    left[:half, :] = two[:half].astype(BF16)
    right[:half, :] = two[half:].astype(BF16)
    three = term(3 * rows, rows)
    held_left[...] = three[:half]
    left[half:, :] = three[half:].astype(BF16)
    one = term(rows, rows)
    right[half:, :] = one[:half].astype(BF16)
    held_right[...] = one[half:]
    own[...] = term(0, rows)


def update_terms(places, mixed, weights, rows):
    width = weights[0].shape[0] // 2
    return pl.pallas_call(
        update_kernel,
        out_shape=[
            like((rows, width), F32),
            like((rows, width), BF16),
            like((rows, width), BF16),
            like((rows // 2, width), F32),
            like((rows // 2, width), F32),
        ],
        in_specs=[SMEM] + [VMEM] * 4 + [ANY] * 4,
        out_specs=[VMEM] * 5,
        scratch_shapes=[
            pltpu.VMEM((width, weights[0].shape[1]), BF16),
            pltpu.SemaphoreType.DMA((2, 8)),
        ],
        compiler_params=memory(24),
    )(places, *mixed, *weights)


def noisy_rows(level, generated, noise):
    return ((1.0 - level) * generated.astype(F32) + level * noise.astype(F32)).astype(BF16)


def generate_kernel(
    places, level, latent, noise, own, from_left, from_right, right_last, left_last, generated, noisy
):
    half = own.shape[0] // 2
    width = own.shape[1] // 4
    for block in range(4):
        columns = slice(block * width, (block + 1) * width)
        source = (lax.rem(places[0] + block, 4) * 2 + places[1]) * width
        source = pl.ds(pl.multiple_of(source, 128), width)
        for rows, near, last in (
            (slice(0, half), from_left, right_last),
            (slice(half, 2 * half), from_right, left_last),
        ):
            update = own[rows, columns] + near[half:, columns].astype(F32)
            update = update + last[:, columns].astype(F32)
            made = (latent[rows, source].astype(F32) + update).astype(BF16)
            generated[rows, columns] = made
            noisy[rows, columns] = noisy_rows(level[0], made, noise[rows, source])


def generate_half(places, level, latent, noise, terms):
    shape = terms[0].shape
    return pl.pallas_call(
        generate_kernel,
        out_shape=[like(shape, BF16), like(shape, BF16)],
        in_specs=[SMEM] * 2 + [VMEM] * 7,
        out_specs=[VMEM] * 2,
        compiler_params=memory(24),
    )(places, level, latent, noise, *terms)


def join_kernel(places, level, own, other, noise, generated, noisy):
    width = own.shape[1] // 4
    for block in range(4):
        columns = slice(block * width, (block + 1) * width)
        pair = lax.rem(places[0] + block, 4) * 2
        here = pl.ds(pl.multiple_of((pair + places[1]) * width, 128), width)
        there = pl.ds(pl.multiple_of((pair + 1 - places[1]) * width, 128), width)
        generated[:, here] = own[:, columns]
        made = other[:, columns]
        generated[:, there] = made
        noisy[:, columns] = noisy_rows(level[0], made, noise[:, there])


def join_halves(places, level, own, other, noise):
    return pl.pallas_call(
        join_kernel,
        out_shape=[like(noise.shape, BF16), like(own.shape, BF16)],
        in_specs=[SMEM] * 2 + [VMEM] * 3,
        out_specs=[VMEM] * 2,
        compiler_params=memory(24),
    )(places, level, own, other, noise)


def half_weight_copies(places, matrix, weight, sems, side, head):
    copies = []
    size = matrix.shape[2] // 8
    for block in range(4):
        first = (lax.rem(places[0] + block, 4) * 2 + side) * size
        rows = pl.ds(pl.multiple_of(first, size), size)
        copies.append(
            pltpu.make_async_copy(
                matrix.at[:, head, rows],
                weight.at[head, :, pl.ds(block * size, size)],
                sems.at[head, block],
            )
        )
    return copies


def head_weight(weight, head):
    return jnp.concatenate([weight[head, kind] for kind in range(weight.shape[1])], axis=1)


def apply_gain(places, side, full, gain):
    size = gain.shape[1] // 8
    for block in range(4):
        first = (lax.rem(places[0] + block, 4) * 2 + side) * size
        part = gain[:, pl.ds(pl.multiple_of(first, 128), size)]
        columns = slice(block * size, (block + 1) * size)
        full[:, columns] = (full[:, columns].astype(F32) * part).astype(BF16)


def row_squares(rows):
    values = rows.astype(F32)
    return jnp.sum(values * values, axis=-1, keepdims=True)


def own_half_kernel(places, *refs):
    parts, refs = refs[:3], refs[3:]
    matrix, gain, total, squares, full, weight, part_sems, sems = refs
    heads = sems.shape[0]
    width = weight.shape[1] * weight.shape[3]
    copies = gather_parts(parts, full, part_sems)
    weights = [
        half_weight_copies(places, matrix, weight, sems, places[1], head)
        for head in range(heads)
    ]
    for group in weights:
        for copy in group:
            copy.start()
    for copy in copies:
        copy.wait()
    squares[...] = jnp.broadcast_to(row_squares(full[...]), squares.shape)
    apply_gain(places, places[1], full, gain)
    for head in range(heads):
        for copy in weights[head]:
            copy.wait()
        columns = slice(head * width, (head + 1) * width)
        total[:, columns] = dot(full[...], head_weight(weight, head))


def project_own_half(places, parts, matrix, gain):
    tokens = sum(part.shape[0] for part in parts)
    heads = matrix.shape[1]
    depth, width = parts[0].shape[1], heads * matrix.shape[0] * matrix.shape[3]
    return pl.pallas_call(
        own_half_kernel,
        out_shape=[like((tokens, width), F32), like((tokens, 128), F32)],
        in_specs=[SMEM] + [ANY] * 4 + [VMEM],
        out_specs=[VMEM] * 2,
        scratch_shapes=[
            pltpu.VMEM((tokens, depth), BF16),
            pltpu.VMEM((heads, matrix.shape[0], depth, matrix.shape[3]), BF16),
            pltpu.SemaphoreType.DMA((3,)),
            pltpu.SemaphoreType.DMA((heads, 4)),
        ],
        compiler_params=memory(32),
    )(places, *parts, matrix, gain)


def score_kernel(places, *refs):
    parts, far_parts, refs = refs[:5], refs[5:7], refs[7:]
    back_source, matrix, total, squares, gain = refs[:5]
    outs = [refs[5:10], refs[10:15]]
    (
        full, far, weight, own_weight, held, back, mixed,
        part_sems, far_sems, sems, own_sems, held_sems, back_sem,
    ) = refs[15:]
    heads = sems.shape[0]
    width = weight.shape[1] * weight.shape[3]
    head_width = width // 3
    tokens = full.shape[0]
    step = tokens // 4
    half = tokens // 2
    copies = gather_parts(far_parts, far, far_sems) + gather_parts(parts, full, part_sems)
    weights = []
    for head in range(heads):
        group = half_weight_copies(places, matrix, own_weight, own_sems, places[1], head)
        group += half_weight_copies(places, matrix, weight, sems, 1 - places[1], head)
        columns = pl.ds(head * width, width)
        for index, (source, target, rows) in enumerate(((0, 0, half), (half, half + step, step))):
            group.append(
                pltpu.make_async_copy(
                    total.at[pl.ds(source, rows), columns],
                    held.at[pl.ds(target, rows), columns],
                    held_sems.at[head, index],
                )
            )
        weights.append(group)
        for copy in group:
            copy.start()
    back_copy = pltpu.make_async_copy(back_source, back, back_sem)
    back_copy.start()
    for copy in copies:
        copy.wait()
    own_squares = jnp.concatenate(
        [squares[:half, :1], row_squares(far[...]), squares[half:, :1]]
    )
    mean = (own_squares + row_squares(full[...])) / (2 * full.shape[1])
    inverse_rms = lax.rsqrt(mean + EPSILON)
    apply_gain(places, 1 - places[1], full, gain)
    apply_gain(places, places[1], far, gain)
    for head in range(heads):
        for copy in weights[head]:
            copy.wait()
        columns = slice(head * width, (head + 1) * width)
        held[half : half + step, columns] = dot(far[...], head_weight(own_weight, head))
        projected = (held[:, columns] + dot(full[...], head_weight(weight, head))) * inverse_rms

        def store(first, rows):
            mixed[first : first + rows.shape[0], head * head_width : (head + 1) * head_width] = rows

        mix_head(
            projected[:, :head_width],
            projected[:, head_width : 2 * head_width],
            projected[:, 2 * head_width :],
            store,
        )
    back_copy.wait()

    def back_part(block, flip):
        pair = (block * 2 + flip) * 2
        return jnp.concatenate([back[pair + places[2]], back[pair + 1 - places[2]]], axis=1)

    for flip, (own, left, right, held_left, held_right) in zip((1, 0), outs):

        def term(block, first):
            start = (block * step + first) % tokens
            matrix_part = back_part(block, flip)
            if start + half <= tokens:
                return dot(mixed[start : start + half, :], matrix_part)
            return jnp.concatenate(
                [
                    dot(mixed[start:tokens, :], matrix_part),
                    dot(mixed[: start + half - tokens, :], matrix_part),
                ]
            )

        left[:half, :] = term(2, 0).astype(BF16)
        left[half:, :] = term(3, half).astype(BF16)
        right[:half, :] = term(2, half).astype(BF16)
        right[half:, :] = term(1, 0).astype(BF16)
        held_left[...] = term(3, 0)
        held_right[...] = term(1, half)
        own[...] = dot(mixed[...], back_part(0, flip))


def score_terms(places, parts, far_parts, matrix, total, squares, back, gain):
    width = total.shape[1]
    tokens = sum(part.shape[0] for part in parts)
    heads = matrix.shape[1]
    depth = parts[0].shape[1]
    columns = 2 * back.shape[2]
    one = [
        like((tokens, columns), F32),
        like((tokens, columns), BF16),
        like((tokens, columns), BF16),
        like((tokens // 2, columns), F32),
        like((tokens // 2, columns), F32),
    ]
    outs = pl.pallas_call(
        score_kernel,
        out_shape=one + one,
        in_specs=[SMEM] + [ANY] * 10 + [VMEM] * 2,
        out_specs=[VMEM] * 10,
        scratch_shapes=[
            pltpu.VMEM((tokens, depth), BF16),
            pltpu.VMEM((tokens // 4, depth), BF16),
            pltpu.VMEM((heads, matrix.shape[0], depth, matrix.shape[3]), BF16),
            pltpu.VMEM((heads, matrix.shape[0], depth, matrix.shape[3]), BF16),
            pltpu.VMEM((tokens, width), F32),
            pltpu.VMEM(back.shape, BF16),
            pltpu.VMEM((tokens, width // 3), BF16),
            pltpu.SemaphoreType.DMA((5,)),
            pltpu.SemaphoreType.DMA((2,)),
            pltpu.SemaphoreType.DMA((heads, 4)),
            pltpu.SemaphoreType.DMA((heads, 4)),
            pltpu.SemaphoreType.DMA((heads, 2)),
            pltpu.SemaphoreType.DMA(()),
        ],
        compiler_params=memory(46),
    )(places, *parts, *far_parts, back, matrix, total, squares, gain)
    return outs[:5], outs[5:]


def unit_reverse(values, gradient, scale):
    width = values.shape[-1]
    inverse = lax.rsqrt(jnp.mean(values * values, axis=-1, keepdims=True) + EPSILON)
    along = jnp.sum(gradient * values, axis=-1, keepdims=True) / width
    return scale * inverse * (gradient - values * (along * inverse * inverse))


def reverse_kernel(projected, gradient, out, key_total, value_total):
    tokens, width = gradient.shape
    query, key = projected[:, :width], projected[:, width : 2 * width]
    scale = width**-0.5
    unit_query = unit_rows(query, LOG2_E * scale).astype(BF16)
    unit_key = unit_rows(key, 1.0).astype(BF16)
    value = projected[:, 2 * width :]
    turned_key = unit_rows(key, 1.0).T.astype(BF16)
    turned_value = value.T.astype(BF16)
    value = value.astype(BF16)
    span = tokens // 3
    for first in range(0, tokens, span):
        rows = slice(first, first + span)
        weights = jnp.exp2(dot(unit_query[rows], turned_key))
        totals = jnp.sum(weights, axis=-1, keepdims=True)
        rounded = weights.astype(BF16)
        raw = dot(rounded, value)
        given = gradient[rows, :].astype(F32)
        draw = (given / totals).astype(BF16)
        dtotals = -jnp.sum(given * raw, axis=-1, keepdims=True) / (totals * totals)
        dweights = dot(draw, turned_value).astype(BF16).astype(F32) + dtotals
        dscores = (dweights * weights).astype(BF16)
        dquery = dot(dscores, unit_key).astype(BF16).astype(F32)
        out[rows, :width] = unit_reverse(query[rows], dquery, scale).astype(BF16)
        key_term = dot(dscores, unit_query[rows], 0, 0)
        value_term = dot(rounded, draw, 0, 0)
        if first == 0:
            key_total[...] = key_term
            value_total[...] = value_term
        else:
            key_total[...] += key_term
            value_total[...] += value_term
    dkey = (LN_2 * key_total[...]).astype(BF16).astype(F32)
    out[:, width : 2 * width] = unit_reverse(key, dkey, 1.0).astype(BF16)
    out[:, 2 * width :] = value_total[...].astype(BF16)


def reverse_head(projected, gradient):
    tokens, width = gradient.shape
    return pl.pallas_call(
        reverse_kernel,
        out_shape=like(projected.shape, BF16),
        in_specs=[VMEM] * 2,
        out_specs=VMEM,
        scratch_shapes=[pltpu.VMEM((tokens, width), F32), pltpu.VMEM((tokens, width), F32)],
        compiler_params=memory(24),
    )(projected, gradient)


def local(latent_in, noise, timestep, gen_gain, gen_qkv, gen_out, score_gain, score_qkv, score_out):
    place = lax.axis_index("fsdp")
    core, x_half, y_place = place % 2, (place // 2) % 2, place // 4
    group = lax.axis_index("group")
    fsdp_size = lax.axis_size("fsdp")
    seq_size = lax.axis_size("seq")
    group_size = lax.axis_size("group")
    head_width = gen_qkv.shape[-1]
    gen_heads = gen_qkv.shape[1]
    model_width = latent_in.shape[2]
    local_rows = latent_in.shape[1]
    places = jnp.stack([y_place, group, core]).astype(jnp.int32)

    fraction = (timestep[0].astype(F32) + 1.0) / STEPS
    noise_level = SHIFT_FACTOR * fraction / (1.0 + (SHIFT_FACTOR - 1.0) * fraction)
    level = noise_level.reshape(1)

    left_z, right_z = seq_ring()
    left_y, right_y = y_ring()
    normed = normalize_turned(latent_in[0], gen_gain, places)
    pair = core_rows(
        [gen_qkv.reshape(gen_qkv.shape[0], -1), gen_out.reshape(gen_out.shape[0], -1)], core
    )
    normed, pair = lax.optimization_barrier((normed, pair))
    right_shard, left_shard = left_z(normed), right_z(normed)
    block = jnp.concatenate(ordered(x_half, pair, swap_half(pair)))
    block, score_qkv = lax.optimization_barrier((block, score_qkv))
    score_matrix = jnp.transpose(score_qkv[:, 0], (2, 1, 0, 3))
    right_shard, left_shard, right_block, left_block, score_matrix = lax.optimization_barrier(
        (right_shard, left_shard, left_y(block), right_y(block), score_matrix)
    )

    half = local_rows // 2
    rows = block.shape[0] // 2
    far_first, far_second, right_far, left_far, right_block, left_block = lax.optimization_barrier(
        (
            left_z(right_shard[:half]),
            right_z(left_shard[half:]),
            left_y(right_block[:rows]),
            right_y(left_block[rows:]),
            right_block,
            left_block,
        )
    )
    own_buffer = jnp.concatenate([block, right_block, right_far, left_far, left_block])
    other_buffer = swap_core(own_buffer)

    out_columns = own_buffer[:, 3 * head_width :]
    out_halves = out_columns.reshape(4, 2, -1, head_width)
    own_heads = swap_group(jnp.where(group == 0, out_halves[:, 1], out_halves[:, 0]))
    own_heads = own_heads.reshape(-1, head_width)

    moves = []
    for g in range(group_size):
        for f in range(fsdp_size):
            for s in range(seq_size):
                source = ((g ^ ((f // 2) % 2)) * fsdp_size + f) * seq_size + (s + f // 4) % seq_size
                moves.append((source, (g * fsdp_size + f) * seq_size + s))
    normed_parts = [normed, right_shard, far_first, far_second, left_shard]
    normed_full, own_projected, own_mixed = first_head(normed_parts, own_buffer)
    own_heads, own_mixed = lax.optimization_barrier((own_heads, own_mixed))
    other_heads = swap_core(own_heads)
    own_partner = swap_group(own_mixed)
    other_projected, other_mixed = next_head(normed_full, other_buffer)
    other_mixed, buffer = lax.optimization_barrier((other_mixed, own_buffer))
    other_partner = swap_group(other_mixed)
    head_columns = lax.ppermute(
        out_columns_in_order(places, buffer, head_width), ("group", "fsdp", "seq"), moves
    )

    terms = update_terms(
        places,
        [own_mixed, own_partner, other_mixed, other_partner],
        [own_buffer, own_heads, other_buffer, other_heads],
        local_rows,
    )
    sums, head_columns = ring_sum(*terms[1:], seq_ring(), head_columns)
    polarity = (2 * group - 1).astype(F32)
    back_block = dot(score_out[:, 0].reshape(model_width, -1), head_columns, 0, 0)
    back_block = (polarity * back_block).astype(BF16)
    back_blocks = lax.all_gather(back_block, "fsdp", axis=0)
    own_made, own_noisy = generate_half(
        places, level, latent_in[0], noise[0], [terms[0], *sums]
    )
    other_made = swap_group(own_made)
    own_parts = ring_gather(own_noisy, seq_ring())
    generated, other_noisy = join_halves(places, level, own_made, other_made, noise[0])
    near_parts = [own_parts[0], own_parts[1], own_parts[4]]
    total, squares = project_own_half(places, near_parts, score_matrix, score_gain)
    right_other, left_other, total = lax.optimization_barrier(
        (left_z(other_noisy), right_z(other_noisy), total)
    )
    other_parts = [
        other_noisy,
        right_other,
        left_z(right_other[:half]),
        right_z(left_other[half:]),
        left_other,
    ]

    flipped, straight = score_terms(
        places, other_parts, own_parts[2:4], score_matrix, total, squares, back_blocks, score_gain
    )

    flipped_sum = ring_total(flipped[0], *ring_sum(*flipped[1:], seq_ring()))
    flipped_sum = swap_group(flipped_sum.astype(BF16))
    dmixed = ring_total(straight[0], *ring_sum(*straight[1:], seq_ring()))
    dmixed = (dmixed + flipped_sum.astype(F32)) * (-noise_level / float(fsdp_size))
    dmixed = dmixed.astype(BF16)

    dother = reverse_head(other_projected, dmixed[:, head_width:])
    sent = dot(normed_full, dother, 0, 0).astype(BF16)
    got = swap_core(sent)
    down = reverse_head(own_projected, dmixed[:, :head_width])
    pair = (dot(normed_full, down, 0, 0) + got.astype(F32)).reshape(4, model_width // 4, -1)
    rows = pair.shape[1] // 2
    summed = ring_total(
        pair[0],
        *ring_sum(
            jnp.concatenate([pair[2, :rows], pair[3, rows:]]).astype(BF16),
            jnp.concatenate([pair[2, rows:], pair[1, :rows]]).astype(BF16),
            pair[3, :rows],
            pair[1, rows:],
            y_ring(),
        ),
    )
    rows = rows // 2

    def rows_of(x, c):
        return lax.dynamic_slice_in_dim(summed, (2 * x + c) * rows, rows)

    over_x = swap_half(rows_of(1 - x_half, core).astype(BF16))
    over_core = swap_core(rows_of(x_half, 1 - core).astype(BF16))
    over_both = lax.ppermute(
        rows_of(1 - x_half, 1 - core).astype(BF16), "fsdp", [(i, i ^ 3) for i in range(fsdp_size)]
    )
    own_head = rows_of(x_half, core) + over_x.astype(F32)
    other_head = over_core.astype(F32) + over_both.astype(F32)
    gen_grad = jnp.concatenate(ordered(core, own_head, other_head), axis=1)
    return (generated[None], gen_grad.reshape(-1, gen_heads, 3, head_width))


def solution(mesh):
    in_specs = (
        P("fsdp", "seq", None),
        P("fsdp", "seq", None),
        P("fsdp"),
        P(),
        P("fsdp", ("group", "seq"), None, None),
        P("fsdp", ("group", "seq"), None),
        P("group", None),
        P(None, "group", "seq", None, None),
        P(None, "group", "seq", None),
    )
    out_specs = (P("fsdp", "seq", None), P("fsdp", ("group", "seq"), None, None))
    return jax.shard_map(local, mesh=mesh, in_specs=in_specs, out_specs=out_specs, check_vma=False)
```

```python
import jax
import jax.numpy as jnp
from jax import lax
from jax.experimental import pallas as pl
from jax.experimental.pallas import tpu as pltpu
from jax.sharding import PartitionSpec as P

STEPS = 1000
SHIFT_FACTOR = 3.0
EPSILON = 1e-06
LOG2_E = 1.4426950408889634
LN_2 = 0.6931471805599453
F32 = jnp.float32
BF16 = jnp.bfloat16
VMEM = pl.BlockSpec(memory_space=pltpu.VMEM)
SMEM = pl.BlockSpec(memory_space=pltpu.SMEM)
ANY = pl.BlockSpec(memory_space=pl.ANY)


def like(shape, dtype):
    return jax.ShapeDtypeStruct(shape, dtype)


def memory(mebibytes):
    return pltpu.CompilerParams(vmem_limit_bytes=mebibytes * 2**20)


def shift(axis, size, stride, step):
    length = lax.axis_size(axis)
    moves = []
    for i in range(length):
        place = (i // stride) % size
        moves.append((i, i + ((place + step) % size - place) * stride))
    return lambda piece: lax.ppermute(piece, axis, moves)


def seq_ring():
    size = lax.axis_size("seq")
    return shift("seq", size, 1, -1), shift("seq", size, 1, 1)


def y_ring():
    size = lax.axis_size("fsdp") // 4
    return shift("fsdp", size, 4, -1), shift("fsdp", size, 4, 1)


def swap_group(piece):
    return shift("group", 2, 1, 1)(piece)


def swap_core(piece):
    return shift("fsdp", 2, 1, 1)(piece)


def swap_half(piece):
    return shift("fsdp", 2, 2, 1)(piece)


def ring_gather(shard, ring):
    to_left, to_right = ring
    half = shard.shape[0] // 2
    right = to_left(shard)
    left = to_right(shard)
    return [shard, right, to_left(right[:half]), to_right(left[half:]), left]


def ring_sum(left_first, right_first, held_left, held_right, ring, beside=None):
    to_left, to_right = ring
    half = held_left.shape[0]
    from_right = to_left(left_first)
    from_left = to_right(right_first)
    if beside is not None:
        from_right, from_left, beside = lax.optimization_barrier((from_right, from_left, beside))
    from_right_last = to_left((held_left + from_right[:half].astype(F32)).astype(BF16))
    from_left_last = to_right((held_right + from_left[:half].astype(F32)).astype(BF16))
    sums = (from_left, from_right, from_right_last, from_left_last)
    return sums if beside is None else (sums, beside)


def ring_total(own, from_left, from_right, from_right_last, from_left_last):
    half = own.shape[0] // 2
    first = own[:half] + from_left[half:].astype(F32) + from_right_last.astype(F32)
    second = own[half:] + from_right[half:].astype(F32) + from_left_last.astype(F32)
    return jnp.concatenate([first, second])


def ordered(flag, own, other):
    first = jnp.where(flag == 0, own, other)
    second = jnp.where(flag == 0, other, own)
    return first, second


def core_rows(shards, core):
    keep, send = [], []
    for shard in shards:
        width = shard.shape[1] // 2
        low, high = shard[:, :width], shard[:, width:]
        keep.append(jnp.where(core == 0, low, high))
        send.append(jnp.where(core == 0, high, low))
    own = jnp.concatenate(keep, axis=1)
    other = swap_core(jnp.concatenate(send, axis=1))
    return jnp.concatenate(ordered(core, own, other))


def normalize_kernel(place_ref, values_ref, gain_ref, out_ref):
    blocks = 4
    width = values_ref.shape[1] // blocks
    values = values_ref[...].astype(F32)
    inverse_rms = lax.rsqrt(jnp.mean(values * values, axis=-1, keepdims=True) + EPSILON)
    for block in range(blocks):
        source = pl.multiple_of(lax.rem(place_ref[0] + block, blocks) * width, 128)
        part = values_ref[:, pl.ds(source, width)].astype(F32)
        out_ref[:, block * width : (block + 1) * width] = (
            part * inverse_rms * gain_ref[:, pl.ds(source, width)]
        ).astype(BF16)


def normalize_turned(values, gain_vector, places):
    return pl.pallas_call(
        normalize_kernel,
        out_shape=like(values.shape, BF16),
        in_specs=[SMEM, VMEM, VMEM],
        out_specs=VMEM,
        compiler_params=memory(16),
    )(places, values, gain_vector[None])


def unit_rows(values, scale):
    mean = jnp.mean(values * values, axis=-1, keepdims=True)
    return values * lax.rsqrt(mean + EPSILON) * scale


def dot(left, right, left_dim=1, right_dim=0):
    return lax.dot_general(
        left, right, (((left_dim,), (right_dim,)), ((), ())), preferred_element_type=F32
    )


def mix_head(query, key, value, store):
    tokens, width = query.shape
    unit_query = unit_rows(query, LOG2_E * width**-0.5).astype(BF16)
    turned_key = unit_rows(key, 1.0).T.astype(BF16)
    value = value.astype(BF16)
    span = tokens // 3
    for first in range(0, tokens, span):
        weights = jnp.exp2(dot(unit_query[first : first + span], turned_key))
        totals = jnp.sum(weights, axis=-1, keepdims=True)
        store(first, (dot(weights.astype(BF16), value) / totals).astype(BF16))


def gather_parts(parts, target, sems):
    copies = []
    row = 0
    for index, part in enumerate(parts):
        rows = part.shape[0]
        copies.append(
            pltpu.make_async_copy(part, target.at[pl.ds(row, rows)], sems.at[index])
        )
        row += rows
    for copy in copies:
        copy.start()
    return copies


def project_mix(full_ref, weight_ref, projected_ref, mixed_ref):
    width = mixed_ref.shape[1]
    projected_ref[...] = dot(full_ref[...], weight_ref[:, : 3 * width])

    def store(first, rows):
        mixed_ref[first : first + rows.shape[0], :] = rows

    mix_head(
        projected_ref[:, :width],
        projected_ref[:, width : 2 * width],
        projected_ref[:, 2 * width :],
        store,
    )


def first_head_kernel(*refs):
    parts, (weight_ref, full_ref, projected_ref, mixed_ref, sems) = refs[:-5], refs[-5:]
    for copy in gather_parts(parts, full_ref, sems):
        copy.wait()
    project_mix(full_ref, weight_ref, projected_ref, mixed_ref)


def head_outputs(tokens, weight):
    width = weight.shape[1] // 4
    return [like((tokens, 3 * width), F32), like((tokens, width), BF16)]


def first_head(parts, weight):
    tokens = sum(part.shape[0] for part in parts)
    return pl.pallas_call(
        first_head_kernel,
        out_shape=[like((tokens, weight.shape[0]), BF16)] + head_outputs(tokens, weight),
        in_specs=[ANY] * len(parts) + [VMEM],
        out_specs=[VMEM] * 3,
        scratch_shapes=[pltpu.SemaphoreType.DMA((len(parts),))],
        compiler_params=memory(60),
    )(*parts, weight)


def next_head(full, weight):
    return pl.pallas_call(
        project_mix,
        out_shape=head_outputs(full.shape[0], weight),
        in_specs=[VMEM] * 2,
        out_specs=[VMEM] * 2,
        compiler_params=memory(32),
    )(full, weight)


def columns_kernel(places, buffer, out, sems):
    rows = out.shape[0] // 4
    first = buffer.shape[1] - out.shape[1]
    copies = []
    for block in range(4):
        place = pl.multiple_of(lax.rem(places[0] + block, 4) * rows, rows)
        copies.append(
            pltpu.make_async_copy(
                buffer.at[pl.ds(block * rows, rows), pl.ds(first, out.shape[1])],
                out.at[pl.ds(place, rows)],
                sems.at[block],
            )
        )
    for copy in copies:
        copy.start()
    for copy in copies:
        copy.wait()


def out_columns_in_order(places, buffer, width):
    return pl.pallas_call(
        columns_kernel,
        out_shape=like((buffer.shape[0], width), BF16),
        in_specs=[SMEM, ANY],
        out_specs=VMEM,
        scratch_shapes=[pltpu.SemaphoreType.DMA((4,))],
        compiler_params=memory(16),
    )(places, buffer)


def update_kernel(
    places, a_own, b_own, a_other, b_other, own_buffer, own_heads, other_buffer, other_heads,
    own, left, right, held_left, held_right, matrix, sems
):
    width = a_own.shape[1]
    size = own.shape[1] // 4
    copies = []
    for side, (buffer, heads) in enumerate(
        ((own_buffer, own_heads), (other_buffer, other_heads))
    ):
        for block in range(4):
            first = pl.multiple_of((2 * block + places[1]) * size, size)
            rows = pl.ds(block * size, size)
            for index, source in enumerate(
                (buffer.at[pl.ds(first, size), pl.ds(3 * width, width)], heads.at[rows])
            ):
                target = matrix.at[rows, pl.ds((2 * side + index) * width, width)]
                copies.append(
                    pltpu.make_async_copy(source, target, sems.at[side, 2 * block + index])
                )
    for copy in copies:
        copy.start()
    for copy in copies:
        copy.wait()
    mixed = jnp.concatenate([a_own[...], b_own[...], a_other[...], b_other[...]], axis=1)
    rows = own.shape[0]
    half = rows // 2

    def term(first, count):
        return dot(mixed[first : first + count], matrix[...], 1, 1)

    two = term(2 * rows, rows)
    left[:half, :] = two[:half].astype(BF16)
    right[:half, :] = two[half:].astype(BF16)
    three = term(3 * rows, rows)
    held_left[...] = three[:half]
    left[half:, :] = three[half:].astype(BF16)
    one = term(rows, rows)
    right[half:, :] = one[:half].astype(BF16)
    held_right[...] = one[half:]
    own[...] = term(0, rows)


def update_terms(places, mixed, weights, rows):
    width = weights[0].shape[0] // 2
    return pl.pallas_call(
        update_kernel,
        out_shape=[
            like((rows, width), F32),
            like((rows, width), BF16),
            like((rows, width), BF16),
            like((rows // 2, width), F32),
            like((rows // 2, width), F32),
        ],
        in_specs=[SMEM] + [VMEM] * 4 + [ANY] * 4,
        out_specs=[VMEM] * 5,
        scratch_shapes=[
            pltpu.VMEM((width, weights[0].shape[1]), BF16),
            pltpu.SemaphoreType.DMA((2, 8)),
        ],
        compiler_params=memory(24),
    )(places, *mixed, *weights)


def noisy_rows(level, generated, noise):
    return ((1.0 - level) * generated.astype(F32) + level * noise.astype(F32)).astype(BF16)


def generate_kernel(
    places, level, latent, noise, own, from_left, from_right, right_last, left_last, generated, noisy
):
    half = own.shape[0] // 2
    width = own.shape[1] // 4
    for block in range(4):
        columns = slice(block * width, (block + 1) * width)
        source = (lax.rem(places[0] + block, 4) * 2 + places[1]) * width
        source = pl.ds(pl.multiple_of(source, 128), width)
        for rows, near, last in (
            (slice(0, half), from_left, right_last),
            (slice(half, 2 * half), from_right, left_last),
        ):
            update = own[rows, columns] + near[half:, columns].astype(F32)
            update = update + last[:, columns].astype(F32)
            made = (latent[rows, source].astype(F32) + update).astype(BF16)
            generated[rows, columns] = made
            noisy[rows, columns] = noisy_rows(level[0], made, noise[rows, source])


def generate_half(places, level, latent, noise, terms):
    shape = terms[0].shape
    return pl.pallas_call(
        generate_kernel,
        out_shape=[like(shape, BF16), like(shape, BF16)],
        in_specs=[SMEM] * 2 + [VMEM] * 7,
        out_specs=[VMEM] * 2,
        compiler_params=memory(24),
    )(places, level, latent, noise, *terms)


def join_kernel(places, level, own, other, noise, generated, noisy):
    width = own.shape[1] // 4
    for block in range(4):
        columns = slice(block * width, (block + 1) * width)
        pair = lax.rem(places[0] + block, 4) * 2
        here = pl.ds(pl.multiple_of((pair + places[1]) * width, 128), width)
        there = pl.ds(pl.multiple_of((pair + 1 - places[1]) * width, 128), width)
        generated[:, here] = own[:, columns]
        made = other[:, columns]
        generated[:, there] = made
        noisy[:, columns] = noisy_rows(level[0], made, noise[:, there])


def join_halves(places, level, own, other, noise):
    return pl.pallas_call(
        join_kernel,
        out_shape=[like(noise.shape, BF16), like(own.shape, BF16)],
        in_specs=[SMEM] * 2 + [VMEM] * 3,
        out_specs=[VMEM] * 2,
        compiler_params=memory(24),
    )(places, level, own, other, noise)


def half_weight_copies(places, matrix, weight, sems, side, head):
    copies = []
    size = matrix.shape[2] // 8
    for block in range(4):
        first = (lax.rem(places[0] + block, 4) * 2 + side) * size
        rows = pl.ds(pl.multiple_of(first, size), size)
        copies.append(
            pltpu.make_async_copy(
                matrix.at[:, head, rows],
                weight.at[head, :, pl.ds(block * size, size)],
                sems.at[head, block],
            )
        )
    return copies


def head_weight(weight, head):
    return jnp.concatenate([weight[head, kind] for kind in range(weight.shape[1])], axis=1)


def apply_gain(places, side, full, gain):
    size = gain.shape[1] // 8
    for block in range(4):
        first = (lax.rem(places[0] + block, 4) * 2 + side) * size
        part = gain[:, pl.ds(pl.multiple_of(first, 128), size)]
        columns = slice(block * size, (block + 1) * size)
        full[:, columns] = (full[:, columns].astype(F32) * part).astype(BF16)


def row_squares(rows):
    values = rows.astype(F32)
    return jnp.sum(values * values, axis=-1, keepdims=True)


def own_half_kernel(places, *refs):
    parts, refs = refs[:3], refs[3:]
    matrix, gain, total, squares, full, weight, part_sems, sems = refs
    heads = sems.shape[0]
    width = weight.shape[1] * weight.shape[3]
    copies = gather_parts(parts, full, part_sems)
    weights = [
        half_weight_copies(places, matrix, weight, sems, places[1], head)
        for head in range(heads)
    ]
    for group in weights:
        for copy in group:
            copy.start()
    for copy in copies:
        copy.wait()
    squares[...] = jnp.broadcast_to(row_squares(full[...]), squares.shape)
    apply_gain(places, places[1], full, gain)
    for head in range(heads):
        for copy in weights[head]:
            copy.wait()
        columns = slice(head * width, (head + 1) * width)
        total[:, columns] = dot(full[...], head_weight(weight, head))


def project_own_half(places, parts, matrix, gain):
    tokens = sum(part.shape[0] for part in parts)
    heads = matrix.shape[1]
    depth, width = parts[0].shape[1], heads * matrix.shape[0] * matrix.shape[3]
    return pl.pallas_call(
        own_half_kernel,
        out_shape=[like((tokens, width), F32), like((tokens, 128), F32)],
        in_specs=[SMEM] + [ANY] * 4 + [VMEM],
        out_specs=[VMEM] * 2,
        scratch_shapes=[
            pltpu.VMEM((tokens, depth), BF16),
            pltpu.VMEM((heads, matrix.shape[0], depth, matrix.shape[3]), BF16),
            pltpu.SemaphoreType.DMA((3,)),
            pltpu.SemaphoreType.DMA((heads, 4)),
        ],
        compiler_params=memory(60),
    )(places, *parts, matrix, gain)


def score_kernel(places, *refs):
    parts, far_parts, refs = refs[:5], refs[5:7], refs[7:]
    back_source, matrix, total, squares, gain = refs[:5]
    outs = [refs[5:10], refs[10:15]]
    (
        full, far, weight, own_weight, held, back, mixed,
        part_sems, far_sems, sems, own_sems, held_sems, back_sem,
    ) = refs[15:]
    heads = sems.shape[0]
    width = weight.shape[1] * weight.shape[3]
    head_width = width // 3
    tokens = full.shape[0]
    step = tokens // 4
    half = tokens // 2
    copies = gather_parts(far_parts, far, far_sems) + gather_parts(parts, full, part_sems)
    weights = []
    for head in range(heads):
        group = half_weight_copies(places, matrix, own_weight, own_sems, places[1], head)
        group += half_weight_copies(places, matrix, weight, sems, 1 - places[1], head)
        columns = pl.ds(head * width, width)
        for index, (source, target, rows) in enumerate(((0, 0, half), (half, half + step, step))):
            group.append(
                pltpu.make_async_copy(
                    total.at[pl.ds(source, rows), columns],
                    held.at[pl.ds(target, rows), columns],
                    held_sems.at[head, index],
                )
            )
        weights.append(group)
        for copy in group:
            copy.start()
    back_copy = pltpu.make_async_copy(back_source, back, back_sem)
    back_copy.start()
    for copy in copies:
        copy.wait()
    own_squares = jnp.concatenate(
        [squares[:half, :1], row_squares(far[...]), squares[half:, :1]]
    )
    mean = (own_squares + row_squares(full[...])) / (2 * full.shape[1])
    inverse_rms = lax.rsqrt(mean + EPSILON)
    apply_gain(places, 1 - places[1], full, gain)
    apply_gain(places, places[1], far, gain)
    for first_head in range(0, heads, 2):
        pair = (first_head, first_head + 1)
        for head in pair:
            for copy in weights[head]:
                copy.wait()
        columns = slice(first_head * width, (first_head + 2) * width)
        here, there = [
            jnp.concatenate([head_weight(each, head) for head in pair], axis=1)
            for each in (own_weight, weight)
        ]
        held[half : half + step, columns] = dot(far[...], here)
        projected = (held[:, columns] + dot(full[...], there)) * inverse_rms
        for head in pair:
            first_lane = (head - first_head) * width
            query, key, value = [
                projected[:, first_lane + kind * head_width : first_lane + (kind + 1) * head_width]
                for kind in range(3)
            ]

            def store(first, rows, head=head):
                lanes = slice(head * head_width, (head + 1) * head_width)
                mixed[first : first + rows.shape[0], lanes] = rows

            mix_head(query, key, value, store)
    back_copy.wait()

    def back_part(block, flip):
        pair = (block * 2 + flip) * 2
        return jnp.concatenate([back[pair + places[2]], back[pair + 1 - places[2]]])

    for flip, (own, left, right, held_left, held_right) in zip((1, 0), outs):

        def term(block):
            start = block * step
            rows = mixed[...]
            if block:
                rows = jnp.concatenate([mixed[start:, :], mixed[:start, :]])
            return dot(rows, back_part(block, flip), 1, 1)

        two = term(2)
        left[:half, :] = two[:half].astype(BF16)
        right[:half, :] = two[half:].astype(BF16)
        three = term(3)
        held_left[...] = three[:half]
        left[half:, :] = three[half:].astype(BF16)
        one = term(1)
        right[half:, :] = one[:half].astype(BF16)
        held_right[...] = one[half:]
        own[...] = term(0)


def score_terms(places, parts, far_parts, matrix, total, squares, back, gain):
    width = total.shape[1]
    tokens = sum(part.shape[0] for part in parts)
    heads = matrix.shape[1]
    depth = parts[0].shape[1]
    columns = 2 * back.shape[1]
    one = [
        like((tokens, columns), F32),
        like((tokens, columns), BF16),
        like((tokens, columns), BF16),
        like((tokens // 2, columns), F32),
        like((tokens // 2, columns), F32),
    ]
    outs = pl.pallas_call(
        score_kernel,
        out_shape=one + one,
        in_specs=[SMEM] + [ANY] * 10 + [VMEM] * 2,
        out_specs=[VMEM] * 10,
        scratch_shapes=[
            pltpu.VMEM((tokens, depth), BF16),
            pltpu.VMEM((tokens // 4, depth), BF16),
            pltpu.VMEM((heads, matrix.shape[0], depth, matrix.shape[3]), BF16),
            pltpu.VMEM((heads, matrix.shape[0], depth, matrix.shape[3]), BF16),
            pltpu.VMEM((tokens, width), F32),
            pltpu.VMEM(back.shape, BF16),
            pltpu.VMEM((tokens, width // 3), BF16),
            pltpu.SemaphoreType.DMA((5,)),
            pltpu.SemaphoreType.DMA((2,)),
            pltpu.SemaphoreType.DMA((heads, 4)),
            pltpu.SemaphoreType.DMA((heads, 4)),
            pltpu.SemaphoreType.DMA((heads, 2)),
            pltpu.SemaphoreType.DMA(()),
        ],
        compiler_params=memory(60),
    )(places, *parts, *far_parts, back, matrix, total, squares, gain)
    return outs[:5], outs[5:]


def unit_reverse(values, gradient, scale):
    width = values.shape[-1]
    inverse = lax.rsqrt(jnp.mean(values * values, axis=-1, keepdims=True) + EPSILON)
    along = jnp.sum(gradient * values, axis=-1, keepdims=True) / width
    return scale * inverse * (gradient - values * (along * inverse * inverse))


def reverse_kernel(projected, gradient, out, key_total, value_total):
    tokens, width = gradient.shape
    query, key = projected[:, :width], projected[:, width : 2 * width]
    scale = width**-0.5
    unit_query = unit_rows(query, LOG2_E * scale).astype(BF16)
    unit_key = unit_rows(key, 1.0).astype(BF16)
    value = projected[:, 2 * width :]
    turned_key = unit_rows(key, 1.0).T.astype(BF16)
    turned_value = value.T.astype(BF16)
    value = value.astype(BF16)
    span = tokens // 3
    for first in range(0, tokens, span):
        rows = slice(first, first + span)
        weights = jnp.exp2(dot(unit_query[rows], turned_key))
        totals = jnp.sum(weights, axis=-1, keepdims=True)
        rounded = weights.astype(BF16)
        raw = dot(rounded, value)
        given = gradient[rows, :].astype(F32)
        draw = (given / totals).astype(BF16)
        dtotals = -jnp.sum(given * raw, axis=-1, keepdims=True) / (totals * totals)
        dweights = dot(draw, turned_value).astype(BF16).astype(F32) + dtotals
        dscores = (dweights * weights).astype(BF16)
        dquery = dot(dscores, unit_key).astype(BF16).astype(F32)
        out[rows, :width] = unit_reverse(query[rows], dquery, scale).astype(BF16)
        key_term = dot(dscores, unit_query[rows], 0, 0)
        value_term = dot(rounded, draw, 0, 0)
        if first == 0:
            key_total[...] = key_term
            value_total[...] = value_term
        else:
            key_total[...] += key_term
            value_total[...] += value_term
    dkey = (LN_2 * key_total[...]).astype(BF16).astype(F32)
    out[:, width : 2 * width] = unit_reverse(key, dkey, 1.0).astype(BF16)
    out[:, 2 * width :] = value_total[...].astype(BF16)


def reverse_head(projected, gradient):
    tokens, width = gradient.shape
    return pl.pallas_call(
        reverse_kernel,
        out_shape=like(projected.shape, BF16),
        in_specs=[VMEM] * 2,
        out_specs=VMEM,
        scratch_shapes=[pltpu.VMEM((tokens, width), F32), pltpu.VMEM((tokens, width), F32)],
        compiler_params=memory(24),
    )(projected, gradient)


def local(latent_in, noise, timestep, gen_gain, gen_qkv, gen_out, score_gain, score_qkv, score_out):
    place = lax.axis_index("fsdp")
    core, x_half, y_place = place % 2, (place // 2) % 2, place // 4
    group = lax.axis_index("group")
    fsdp_size = lax.axis_size("fsdp")
    seq_size = lax.axis_size("seq")
    group_size = lax.axis_size("group")
    head_width = gen_qkv.shape[-1]
    gen_heads = gen_qkv.shape[1]
    model_width = latent_in.shape[2]
    local_rows = latent_in.shape[1]
    places = jnp.stack([y_place, group, core]).astype(jnp.int32)

    fraction = (timestep[0].astype(F32) + 1.0) / STEPS
    noise_level = SHIFT_FACTOR * fraction / (1.0 + (SHIFT_FACTOR - 1.0) * fraction)
    level = noise_level.reshape(1)

    left_z, right_z = seq_ring()
    left_y, right_y = y_ring()
    normed = normalize_turned(latent_in[0], gen_gain, places)
    pair = core_rows(
        [gen_qkv.reshape(gen_qkv.shape[0], -1), gen_out.reshape(gen_out.shape[0], -1)], core
    )
    normed, pair = lax.optimization_barrier((normed, pair))
    right_shard, left_shard = left_z(normed), right_z(normed)
    block = jnp.concatenate(ordered(x_half, pair, swap_half(pair)))
    block, score_qkv = lax.optimization_barrier((block, score_qkv))
    score_matrix = jnp.transpose(score_qkv[:, 0], (2, 1, 0, 3))
    right_block, left_block = left_y(block), right_y(block)
    right_shard, left_shard, score_matrix = lax.optimization_barrier(
        (right_shard, left_shard, score_matrix)
    )

    half = local_rows // 2
    rows = block.shape[0] // 2
    far_first, far_second, right_far, left_far, right_block, left_block = lax.optimization_barrier(
        (
            left_z(right_shard[:half]),
            right_z(left_shard[half:]),
            left_y(right_block[:rows]),
            right_y(left_block[rows:]),
            right_block,
            left_block,
        )
    )
    own_buffer = jnp.concatenate([block, right_block, right_far, left_far, left_block])
    other_buffer = swap_core(own_buffer)

    out_columns = own_buffer[:, 3 * head_width :]
    out_halves = out_columns.reshape(4, 2, -1, head_width)
    own_heads = swap_group(jnp.where(group == 0, out_halves[:, 1], out_halves[:, 0]))
    own_heads = own_heads.reshape(-1, head_width)

    moves = []
    for g in range(group_size):
        for f in range(fsdp_size):
            for s in range(seq_size):
                source = ((g ^ ((f // 2) % 2)) * fsdp_size + f) * seq_size + (s + f // 4) % seq_size
                moves.append((source, (g * fsdp_size + f) * seq_size + s))
    normed_parts = [normed, right_shard, far_first, far_second, left_shard]
    normed_full, own_projected, own_mixed = first_head(normed_parts, own_buffer)
    own_heads, own_mixed = lax.optimization_barrier((own_heads, own_mixed))
    other_heads = swap_core(own_heads)
    own_partner = swap_group(own_mixed)
    other_projected, other_mixed = next_head(normed_full, other_buffer)
    other_mixed, buffer = lax.optimization_barrier((other_mixed, own_buffer))
    other_partner = swap_group(other_mixed)
    head_columns = lax.ppermute(
        out_columns_in_order(places, buffer, head_width), ("group", "fsdp", "seq"), moves
    )

    terms = update_terms(
        places,
        [own_mixed, own_partner, other_mixed, other_partner],
        [own_buffer, own_heads, other_buffer, other_heads],
        local_rows,
    )
    sums, head_columns = ring_sum(*terms[1:], seq_ring(), head_columns)
    polarity = (2 * group - 1).astype(F32)
    back_block = dot(head_columns, score_out[:, 0].reshape(model_width, -1), 0, 0)
    back_block = (polarity * back_block).astype(BF16)
    back_blocks = lax.all_gather(back_block, "fsdp", axis=0)
    own_made, own_noisy = generate_half(
        places, level, latent_in[0], noise[0], [terms[0], *sums]
    )
    other_made = swap_group(own_made)
    own_parts = ring_gather(own_noisy, seq_ring())
    generated, other_noisy = join_halves(places, level, own_made, other_made, noise[0])
    near_parts = [own_parts[0], own_parts[1], own_parts[4]]
    total, squares = project_own_half(places, near_parts, score_matrix, score_gain)
    right_other, left_other, total = lax.optimization_barrier(
        (left_z(other_noisy), right_z(other_noisy), total)
    )
    other_parts = [
        other_noisy,
        right_other,
        left_z(right_other[:half]),
        right_z(left_other[half:]),
        left_other,
    ]

    flipped, straight = score_terms(
        places, other_parts, own_parts[2:4], score_matrix, total, squares, back_blocks, score_gain
    )

    flipped_sum = ring_total(flipped[0], *ring_sum(*flipped[1:], seq_ring()))
    flipped_sum = swap_group(flipped_sum.astype(BF16))
    dmixed = ring_total(straight[0], *ring_sum(*straight[1:], seq_ring()))
    dmixed = (dmixed + flipped_sum.astype(F32)) * (-noise_level / float(fsdp_size))
    dmixed = dmixed.astype(BF16)

    dother = reverse_head(other_projected, dmixed[:, head_width:])
    sent = dot(normed_full, dother, 0, 0).astype(BF16)
    got = swap_core(sent)
    down = reverse_head(own_projected, dmixed[:, :head_width])
    pair = (dot(normed_full, down, 0, 0) + got.astype(F32)).reshape(4, model_width // 4, -1)
    rows = pair.shape[1] // 2
    summed = ring_total(
        pair[0],
        *ring_sum(
            jnp.concatenate([pair[2, :rows], pair[3, rows:]]).astype(BF16),
            jnp.concatenate([pair[2, rows:], pair[1, :rows]]).astype(BF16),
            pair[3, :rows],
            pair[1, rows:],
            y_ring(),
        ),
    )
    rows = rows // 2

    def rows_of(x, c):
        return lax.dynamic_slice_in_dim(summed, (2 * x + c) * rows, rows)

    over_x = swap_half(rows_of(1 - x_half, core).astype(BF16))
    over_core = swap_core(rows_of(x_half, 1 - core).astype(BF16))
    over_both = lax.ppermute(
        rows_of(1 - x_half, 1 - core).astype(BF16), "fsdp", [(i, i ^ 3) for i in range(fsdp_size)]
    )
    own_head = rows_of(x_half, core) + over_x.astype(F32)
    other_head = over_core.astype(F32) + over_both.astype(F32)
    gen_grad = jnp.concatenate(ordered(core, own_head, other_head), axis=1)
    return (generated[None], gen_grad.reshape(-1, gen_heads, 3, head_width))


def solution(mesh):
    in_specs = (
        P("fsdp", "seq", None),
        P("fsdp", "seq", None),
        P("fsdp"),
        P(),
        P("fsdp", ("group", "seq"), None, None),
        P("fsdp", ("group", "seq"), None),
        P("group", None),
        P(None, "group", "seq", None, None),
        P(None, "group", "seq", None),
    )
    out_specs = (P("fsdp", "seq", None), P("fsdp", ("group", "seq"), None, None))
    return jax.shard_map(local, mesh=mesh, in_specs=in_specs, out_specs=out_specs, check_vma=False)
```

```python
import functools

import jax
import jax.numpy as jnp
from jax import lax
from jax.experimental import pallas as pl
from jax.experimental.pallas import tpu as pltpu
from jax.sharding import PartitionSpec as P

STEPS = 1000
SHIFT_FACTOR = 3.0
EPSILON = 1e-06
LOG2_E = 1.4426950408889634
LN_2 = 0.6931471805599453
F32 = jnp.float32
BF16 = jnp.bfloat16
VMEM = pl.BlockSpec(memory_space=pltpu.VMEM)
SMEM = pl.BlockSpec(memory_space=pltpu.SMEM)
ANY = pl.BlockSpec(memory_space=pl.ANY)


def like(shape, dtype):
    return jax.ShapeDtypeStruct(shape, dtype)


def memory(mebibytes):
    return pltpu.CompilerParams(vmem_limit_bytes=mebibytes * 2**20)


def shift(axis, size, stride, step):
    length = lax.axis_size(axis)
    moves = []
    for i in range(length):
        place = (i // stride) % size
        moves.append((i, i + ((place + step) % size - place) * stride))
    return lambda piece: lax.ppermute(piece, axis, moves)


def seq_ring():
    size = lax.axis_size("seq")
    return shift("seq", size, 1, -1), shift("seq", size, 1, 1)


def y_ring():
    size = lax.axis_size("fsdp") // 4
    return shift("fsdp", size, 4, -1), shift("fsdp", size, 4, 1)


def swap_group(piece):
    return shift("group", 2, 1, 1)(piece)


def swap_core(piece):
    return shift("fsdp", 2, 1, 1)(piece)


def swap_half(piece):
    return shift("fsdp", 2, 2, 1)(piece)


def ring_gather(shard, ring):
    to_left, to_right = ring
    half = shard.shape[0] // 2
    right = to_left(shard)
    left = to_right(shard)
    return [shard, right, to_left(right[:half]), to_right(left[half:]), left]


def ring_sum(left_first, right_first, held_left, held_right, ring, beside=None):
    to_left, to_right = ring
    half = held_left.shape[0]
    from_right = to_left(left_first)
    from_left = to_right(right_first)
    if beside is not None:
        from_right, from_left, beside = lax.optimization_barrier((from_right, from_left, beside))
    from_right_last = to_left((held_left + from_right[:half].astype(F32)).astype(BF16))
    from_left_last = to_right((held_right + from_left[:half].astype(F32)).astype(BF16))
    sums = (from_left, from_right, from_right_last, from_left_last)
    return sums if beside is None else (sums, beside)


def ring_total(own, from_left, from_right, from_right_last, from_left_last):
    half = own.shape[0] // 2
    first = own[:half] + from_left[half:].astype(F32) + from_right_last.astype(F32)
    second = own[half:] + from_right[half:].astype(F32) + from_left_last.astype(F32)
    return jnp.concatenate([first, second])


def ordered(flag, own, other):
    first = jnp.where(flag == 0, own, other)
    second = jnp.where(flag == 0, other, own)
    return first, second


def core_rows(shards, core):
    keep, send = [], []
    for shard in shards:
        width = shard.shape[1] // 2
        low, high = shard[:, :width], shard[:, width:]
        keep.append(jnp.where(core == 0, low, high))
        send.append(jnp.where(core == 0, high, low))
    own = jnp.concatenate(keep, axis=1)
    other = swap_core(jnp.concatenate(send, axis=1))
    return jnp.concatenate(ordered(core, own, other))


def normalize_kernel(place_ref, values_ref, gain_ref, out_ref):
    blocks = 4
    width = values_ref.shape[1] // blocks
    values = values_ref[...].astype(F32)
    inverse_rms = lax.rsqrt(jnp.mean(values * values, axis=-1, keepdims=True) + EPSILON)
    for block in range(blocks):
        source = pl.multiple_of(lax.rem(place_ref[0] + block, blocks) * width, 128)
        part = values_ref[:, pl.ds(source, width)].astype(F32)
        out_ref[:, block * width : (block + 1) * width] = (
            part * inverse_rms * gain_ref[:, pl.ds(source, width)]
        ).astype(BF16)


def normalize_turned(values, gain_vector, places):
    return pl.pallas_call(
        normalize_kernel,
        out_shape=like(values.shape, BF16),
        in_specs=[SMEM, VMEM, VMEM],
        out_specs=VMEM,
        compiler_params=memory(16),
    )(places, values, gain_vector[None])


def unit_rows(values, scale):
    mean = jnp.mean(values * values, axis=-1, keepdims=True)
    return values * lax.rsqrt(mean + EPSILON) * scale


def dot(left, right, left_dim=1, right_dim=0):
    return lax.dot_general(
        left, right, (((left_dim,), (right_dim,)), ((), ())), preferred_element_type=F32
    )


def loop(count, body):
    lax.fori_loop(0, count, lambda index, carry: (body(index), carry)[1], 0)


def mix_scratch(tokens, width):
    return [
        pltpu.VMEM((tokens, width), BF16),
        pltpu.VMEM((width, tokens), BF16),
        pltpu.VMEM((tokens, width), BF16),
    ]


def mix_head(query, key, value, scratch, store):
    tokens, width = query.shape
    unit_query, turned_key, rounded = scratch
    unit_query[...] = unit_rows(query, LOG2_E * width**-0.5).astype(BF16)
    turned_key[...] = unit_rows(key, 1.0).T.astype(BF16)
    rounded[...] = value.astype(BF16)
    span = tokens // 3

    def mix(index):
        first = pl.multiple_of(index * span, span)
        weights = jnp.exp2(dot(unit_query[pl.ds(first, span), :], turned_key[...]))
        totals = jnp.sum(weights, axis=-1, keepdims=True)
        store(first, (dot(weights.astype(BF16), rounded[...]) / totals).astype(BF16))

    loop(3, mix)


def gather_parts(parts, target, sems):
    copies = []
    row = 0
    for index, part in enumerate(parts):
        rows = part.shape[0]
        copies.append(
            pltpu.make_async_copy(part, target.at[pl.ds(row, rows)], sems.at[index])
        )
        row += rows
    for copy in copies:
        copy.start()
    return copies


def head_kernel(count, *refs):
    parts, refs = refs[:count], refs[count:]
    buffer, projected, mixed, full, weight, query, key, value, sems, weight_sem = refs
    width = mixed.shape[1]
    copies = [
        pltpu.make_async_copy(buffer.at[:, pl.ds(0, 3 * width)], weight, weight_sem)
    ]
    copies[0].start()
    copies += gather_parts(parts, full, sems)
    for copy in copies:
        copy.wait()
    span = full.shape[0] // 3

    def project(index):
        rows = pl.ds(pl.multiple_of(index * span, span), span)
        projected[rows, :] = dot(full[rows, :], weight[...])

    loop(3, project)

    def store(first, rows):
        mixed[pl.ds(first, rows.shape[0]), :] = rows

    mix_head(
        projected[:, :width],
        projected[:, width : 2 * width],
        projected[:, 2 * width :],
        (query, key, value),
        store,
    )


def generator_head(parts, buffer, keep):
    tokens = sum(part.shape[0] for part in parts)
    depth, width = buffer.shape[0], buffer.shape[1] // 4
    outs = [like((tokens, 3 * width), F32), like((tokens, width), BF16)]
    scratch = [pltpu.VMEM((depth, 3 * width), BF16)] + mix_scratch(tokens, width)
    scratch += [pltpu.SemaphoreType.DMA((len(parts),)), pltpu.SemaphoreType.DMA(())]
    if keep:
        outs.append(like((tokens, depth), BF16))
    else:
        scratch.insert(0, pltpu.VMEM((tokens, depth), BF16))
    return pl.pallas_call(
        functools.partial(head_kernel, len(parts)),
        out_shape=outs,
        in_specs=[ANY] * (len(parts) + 1),
        out_specs=[VMEM] * len(outs),
        scratch_shapes=scratch,
        compiler_params=memory(40),
    )(*parts, buffer)


def columns_kernel(places, buffer, out, sems):
    rows = out.shape[0] // 4
    first = buffer.shape[1] - out.shape[1]
    copies = []
    for block in range(4):
        place = pl.multiple_of(lax.rem(places[0] + block, 4) * rows, rows)
        copies.append(
            pltpu.make_async_copy(
                buffer.at[pl.ds(block * rows, rows), pl.ds(first, out.shape[1])],
                out.at[pl.ds(place, rows)],
                sems.at[block],
            )
        )
    for copy in copies:
        copy.start()
    for copy in copies:
        copy.wait()


def out_columns_in_order(places, buffer, width):
    return pl.pallas_call(
        columns_kernel,
        out_shape=like((buffer.shape[0], width), BF16),
        in_specs=[SMEM, ANY],
        out_specs=VMEM,
        scratch_shapes=[pltpu.SemaphoreType.DMA((4,))],
        compiler_params=memory(16),
    )(places, buffer)


def update_kernel(
    places, a_own, b_own, a_other, b_other, own_buffer, own_heads, other_buffer, other_heads,
    own, left, right, held_left, held_right, matrix, whole, sems
):
    width = a_own.shape[1]
    size = own.shape[1] // 4
    copies = []
    for side, (buffer, heads) in enumerate(
        ((own_buffer, own_heads), (other_buffer, other_heads))
    ):
        for block in range(4):
            first = pl.multiple_of((2 * block + places[1]) * size, size)
            rows = pl.ds(block * size, size)
            for index, source in enumerate(
                (buffer.at[pl.ds(first, size), pl.ds(3 * width, width)], heads.at[rows])
            ):
                target = matrix.at[rows, pl.ds((2 * side + index) * width, width)]
                copies.append(
                    pltpu.make_async_copy(source, target, sems.at[side, 2 * block + index])
                )
    for copy in copies:
        copy.start()
    for copy in copies:
        copy.wait()
    whole[...] = jnp.concatenate([a_own[...], b_own[...], a_other[...], b_other[...]], axis=1)
    rows = own.shape[0]
    half = rows // 2

    def block_terms(block):
        first = pl.multiple_of(block * size, size)
        columns = pl.ds(first, size)
        part = matrix[pl.ds(first, size), :]
        terms = dot(whole[...], part, 1, 1)
        own[:, columns] = terms[:rows]
        right[half:, columns] = terms[rows : rows + half].astype(BF16)
        held_right[:, columns] = terms[rows + half : 2 * rows]
        left[:half, columns] = terms[2 * rows : 2 * rows + half].astype(BF16)
        right[:half, columns] = terms[2 * rows + half : 3 * rows].astype(BF16)
        held_left[:, columns] = terms[3 * rows : 3 * rows + half]
        left[half:, columns] = terms[3 * rows + half :].astype(BF16)

    loop(4, block_terms)


def update_terms(places, mixed, weights, rows):
    width = weights[0].shape[0] // 2
    return pl.pallas_call(
        update_kernel,
        out_shape=[
            like((rows, width), F32),
            like((rows, width), BF16),
            like((rows, width), BF16),
            like((rows // 2, width), F32),
            like((rows // 2, width), F32),
        ],
        in_specs=[SMEM] + [VMEM] * 4 + [ANY] * 4,
        out_specs=[VMEM] * 5,
        scratch_shapes=[
            pltpu.VMEM((width, weights[0].shape[1]), BF16),
            pltpu.VMEM((4 * rows, weights[0].shape[1]), BF16),
            pltpu.SemaphoreType.DMA((2, 8)),
        ],
        compiler_params=memory(24),
    )(places, *mixed, *weights)


def noisy_rows(level, generated, noise):
    return ((1.0 - level) * generated.astype(F32) + level * noise.astype(F32)).astype(BF16)


def generate_kernel(
    places, level, latent, noise, own, from_left, from_right, right_last, left_last, generated, noisy
):
    half = own.shape[0] // 2
    width = own.shape[1] // 4
    for block in range(4):
        columns = slice(block * width, (block + 1) * width)
        source = (lax.rem(places[0] + block, 4) * 2 + places[1]) * width
        source = pl.ds(pl.multiple_of(source, 128), width)
        for rows, near, last in (
            (slice(0, half), from_left, right_last),
            (slice(half, 2 * half), from_right, left_last),
        ):
            update = own[rows, columns] + near[half:, columns].astype(F32)
            update = update + last[:, columns].astype(F32)
            made = (latent[rows, source].astype(F32) + update).astype(BF16)
            generated[rows, columns] = made
            noisy[rows, columns] = noisy_rows(level[0], made, noise[rows, source])


def generate_half(places, level, latent, noise, terms):
    shape = terms[0].shape
    return pl.pallas_call(
        generate_kernel,
        out_shape=[like(shape, BF16), like(shape, BF16)],
        in_specs=[SMEM] * 2 + [VMEM] * 7,
        out_specs=[VMEM] * 2,
        compiler_params=memory(24),
    )(places, level, latent, noise, *terms)


def join_kernel(places, level, own, other, noise, generated, noisy):
    width = own.shape[1] // 4
    for block in range(4):
        columns = slice(block * width, (block + 1) * width)
        pair = lax.rem(places[0] + block, 4) * 2
        here = pl.ds(pl.multiple_of((pair + places[1]) * width, 128), width)
        there = pl.ds(pl.multiple_of((pair + 1 - places[1]) * width, 128), width)
        generated[:, here] = own[:, columns]
        made = other[:, columns]
        generated[:, there] = made
        noisy[:, columns] = noisy_rows(level[0], made, noise[:, there])


def join_halves(places, level, own, other, noise):
    return pl.pallas_call(
        join_kernel,
        out_shape=[like(noise.shape, BF16), like(own.shape, BF16)],
        in_specs=[SMEM] * 2 + [VMEM] * 3,
        out_specs=[VMEM] * 2,
        compiler_params=memory(24),
    )(places, level, own, other, noise)


def half_weight_copies(places, matrix, weight, sems, side, head):
    copies = []
    size = matrix.shape[2] // 8
    for block in range(4):
        first = (lax.rem(places[0] + block, 4) * 2 + side) * size
        rows = pl.ds(pl.multiple_of(first, size), size)
        copies.append(
            pltpu.make_async_copy(
                matrix.at[:, head, rows],
                weight.at[head, :, pl.ds(block * size, size)],
                sems.at[head, block],
            )
        )
    return copies


def head_weight(weight, head):
    return jnp.concatenate([weight[head, kind] for kind in range(weight.shape[1])], axis=1)


def scale_rows(places, side, full, gain, squares):
    size = gain.shape[1] // 8
    span = 96

    def scale(index):
        rows = pl.ds(pl.multiple_of(index * span, span), span)
        values = full[rows, :].astype(F32)
        sums = jnp.sum(values * values, axis=-1, keepdims=True)
        squares[rows, :] = jnp.broadcast_to(sums, (span, squares.shape[1]))
        for block in range(4):
            first = (lax.rem(places[0] + block, 4) * 2 + side) * size
            part = gain[:, pl.ds(pl.multiple_of(first, 128), size)]
            columns = slice(block * size, (block + 1) * size)
            full[rows, columns] = (values[:, columns] * part).astype(BF16)

    loop(full.shape[0] // span, scale)


def own_half_kernel(places, *refs):
    parts, refs = refs[:3], refs[3:]
    matrix, gain, total, squares, full, weight, part_sems, sems = refs
    heads = sems.shape[0]
    width = weight.shape[1] * weight.shape[3]
    copies = gather_parts(parts, full, part_sems)
    for head in range(heads):
        for copy in half_weight_copies(places, matrix, weight, sems, places[1], head):
            copy.start()
    for copy in copies:
        copy.wait()
    scale_rows(places, places[1], full, gain, squares)

    def project(head):
        for copy in half_weight_copies(places, matrix, weight, sems, places[1], head):
            copy.wait()
        columns = pl.ds(pl.multiple_of(head * width, 128), width)
        total[:, columns] = dot(full[...], head_weight(weight, head))

    loop(heads, project)


def project_own_half(places, parts, matrix, gain):
    tokens = sum(part.shape[0] for part in parts)
    heads = matrix.shape[1]
    depth, width = parts[0].shape[1], heads * matrix.shape[0] * matrix.shape[3]
    return pl.pallas_call(
        own_half_kernel,
        out_shape=[like((tokens, width), F32), like((tokens, 128), F32)],
        in_specs=[SMEM] + [ANY] * 4 + [VMEM],
        out_specs=[VMEM] * 2,
        scratch_shapes=[
            pltpu.VMEM((tokens, depth), BF16),
            pltpu.VMEM((heads, matrix.shape[0], depth, matrix.shape[3]), BF16),
            pltpu.SemaphoreType.DMA((3,)),
            pltpu.SemaphoreType.DMA((heads, 4)),
        ],
        compiler_params=memory(60),
    )(places, *parts, matrix, gain)


def score_kernel(places, *refs):
    parts, far_parts, refs = refs[:5], refs[5:7], refs[7:]
    back_source, matrix, total, squares, gain = refs[:5]
    outs = [refs[5:10], refs[10:15]]
    (
        full, far, weight, own_weight, held, back, mixed, other_squares, far_squares, inverse_rms,
        query, key, value, part_sems, far_sems, sems, own_sems, held_sems, back_sem,
    ) = refs[15:]
    heads = sems.shape[0]
    width = weight.shape[1] * weight.shape[3]
    head_width = width // 3
    tokens = full.shape[0]
    step = tokens // 4
    half = tokens // 2

    def head_copies(head):
        group = half_weight_copies(places, matrix, own_weight, own_sems, places[1], head)
        group += half_weight_copies(places, matrix, weight, sems, 1 - places[1], head)
        columns = pl.ds(pl.multiple_of(head * width, 128), width)
        for index, (source, target, rows) in enumerate(((0, 0, half), (half, half + step, step))):
            group.append(
                pltpu.make_async_copy(
                    total.at[pl.ds(source, rows), columns],
                    held.at[pl.ds(target, rows), columns],
                    held_sems.at[head, index],
                )
            )
        return group

    copies = gather_parts(far_parts, far, far_sems) + gather_parts(parts, full, part_sems)
    for head in range(heads):
        for copy in head_copies(head):
            copy.start()
    back_copy = pltpu.make_async_copy(back_source, back, back_sem)
    back_copy.start()
    for copy in copies:
        copy.wait()
    scale_rows(places, 1 - places[1], full, gain, other_squares)
    scale_rows(places, places[1], far, gain, far_squares)
    for first, rows, source in (
        (0, half, squares[:half, :]),
        (half, step, far_squares[...]),
        (half + step, step, squares[half:, :]),
    ):
        span = slice(first, first + rows)
        mean = (source + other_squares[span, :]) / (2 * full.shape[1])
        inverse_rms[span, :] = lax.rsqrt(mean + EPSILON)

    def one_head(head):
        for copy in head_copies(head):
            copy.wait()
        columns = pl.ds(pl.multiple_of(head * width, 128), width)
        held[half : half + step, columns] = dot(far[...], head_weight(own_weight, head))
        projected = held[:, columns] + dot(full[...], head_weight(weight, head))
        lanes = pl.ds(pl.multiple_of(head * head_width, 128), head_width)

        def store(first, rows):
            mixed[pl.ds(first, rows.shape[0]), lanes] = rows

        mix_head(
            *[
                projected[:, kind * head_width : (kind + 1) * head_width] * inverse_rms[...]
                for kind in range(3)
            ],
            (query, key, value),
            store,
        )

    loop(heads, one_head)
    back_copy.wait()

    def back_part(block, flip):
        pair = (block * 2 + flip) * 2
        return jnp.concatenate([back[pair + places[2]], back[pair + 1 - places[2]]])

    for flip, (own, left, right, held_left, held_right) in zip((1, 0), outs):

        def term(block):
            start = block * step
            rows = mixed[...]
            if block:
                rows = jnp.concatenate([mixed[start:, :], mixed[:start, :]])
            return dot(rows, back_part(block, flip), 1, 1)

        two = term(2)
        left[:half, :] = two[:half].astype(BF16)
        right[:half, :] = two[half:].astype(BF16)
        three = term(3)
        held_left[...] = three[:half]
        left[half:, :] = three[half:].astype(BF16)
        one = term(1)
        right[half:, :] = one[:half].astype(BF16)
        held_right[...] = one[half:]
        own[...] = term(0)


def score_terms(places, parts, far_parts, matrix, total, squares, back, gain):
    width = total.shape[1]
    tokens = sum(part.shape[0] for part in parts)
    heads = matrix.shape[1]
    depth = parts[0].shape[1]
    columns = 2 * back.shape[1]
    one = [
        like((tokens, columns), F32),
        like((tokens, columns), BF16),
        like((tokens, columns), BF16),
        like((tokens // 2, columns), F32),
        like((tokens // 2, columns), F32),
    ]
    outs = pl.pallas_call(
        score_kernel,
        out_shape=one + one,
        in_specs=[SMEM] + [ANY] * 10 + [VMEM] * 2,
        out_specs=[VMEM] * 10,
        scratch_shapes=[
            pltpu.VMEM((tokens, depth), BF16),
            pltpu.VMEM((tokens // 4, depth), BF16),
            pltpu.VMEM((heads, matrix.shape[0], depth, matrix.shape[3]), BF16),
            pltpu.VMEM((heads, matrix.shape[0], depth, matrix.shape[3]), BF16),
            pltpu.VMEM((tokens, width), F32),
            pltpu.VMEM(back.shape, BF16),
            pltpu.VMEM((tokens, width // 3), BF16),
            pltpu.VMEM((tokens, 128), F32),
            pltpu.VMEM((tokens // 4, 128), F32),
            pltpu.VMEM((tokens, 128), F32),
            *mix_scratch(tokens, matrix.shape[3]),
            pltpu.SemaphoreType.DMA((5,)),
            pltpu.SemaphoreType.DMA((2,)),
            pltpu.SemaphoreType.DMA((heads, 4)),
            pltpu.SemaphoreType.DMA((heads, 4)),
            pltpu.SemaphoreType.DMA((heads, 2)),
            pltpu.SemaphoreType.DMA(()),
        ],
        compiler_params=memory(60),
    )(places, *parts, *far_parts, back, matrix, total, squares, gain)
    return outs[:5], outs[5:]


def unit_reverse(values, gradient, scale):
    width = values.shape[-1]
    inverse = lax.rsqrt(jnp.mean(values * values, axis=-1, keepdims=True) + EPSILON)
    along = jnp.sum(gradient * values, axis=-1, keepdims=True) / width
    return scale * inverse * (gradient - values * (along * inverse * inverse))


def reverse_kernel(projected, gradient, out, key_total, value_total):
    tokens, width = gradient.shape
    query, key = projected[:, :width], projected[:, width : 2 * width]
    scale = width**-0.5
    unit_query = unit_rows(query, LOG2_E * scale).astype(BF16)
    unit_key = unit_rows(key, 1.0).astype(BF16)
    value = projected[:, 2 * width :]
    turned_key = unit_rows(key, 1.0).T.astype(BF16)
    turned_value = value.T.astype(BF16)
    value = value.astype(BF16)
    span = tokens // 3
    for first in range(0, tokens, span):
        rows = slice(first, first + span)
        weights = jnp.exp2(dot(unit_query[rows], turned_key))
        totals = jnp.sum(weights, axis=-1, keepdims=True)
        rounded = weights.astype(BF16)
        raw = dot(rounded, value)
        given = gradient[rows, :].astype(F32)
        draw = (given / totals).astype(BF16)
        dtotals = -jnp.sum(given * raw, axis=-1, keepdims=True) / (totals * totals)
        dweights = dot(draw, turned_value).astype(BF16).astype(F32) + dtotals
        dscores = (dweights * weights).astype(BF16)
        dquery = dot(dscores, unit_key).astype(BF16).astype(F32)
        out[rows, :width] = unit_reverse(query[rows], dquery, scale).astype(BF16)
        key_term = dot(dscores, unit_query[rows], 0, 0)
        value_term = dot(rounded, draw, 0, 0)
        if first == 0:
            key_total[...] = key_term
            value_total[...] = value_term
        else:
            key_total[...] += key_term
            value_total[...] += value_term
    dkey = (LN_2 * key_total[...]).astype(BF16).astype(F32)
    out[:, width : 2 * width] = unit_reverse(key, dkey, 1.0).astype(BF16)
    out[:, 2 * width :] = value_total[...].astype(BF16)


def reverse_head(projected, gradient):
    tokens, width = gradient.shape
    return pl.pallas_call(
        reverse_kernel,
        out_shape=like(projected.shape, BF16),
        in_specs=[VMEM] * 2,
        out_specs=VMEM,
        scratch_shapes=[pltpu.VMEM((tokens, width), F32), pltpu.VMEM((tokens, width), F32)],
        compiler_params=memory(24),
    )(projected, gradient)


def local(latent_in, noise, timestep, gen_gain, gen_qkv, gen_out, score_gain, score_qkv, score_out):
    place = lax.axis_index("fsdp")
    core, x_half, y_place = place % 2, (place // 2) % 2, place // 4
    group = lax.axis_index("group")
    fsdp_size = lax.axis_size("fsdp")
    seq_size = lax.axis_size("seq")
    group_size = lax.axis_size("group")
    head_width = gen_qkv.shape[-1]
    gen_heads = gen_qkv.shape[1]
    model_width = latent_in.shape[2]
    local_rows = latent_in.shape[1]
    places = jnp.stack([y_place, group, core]).astype(jnp.int32)

    fraction = (timestep[0].astype(F32) + 1.0) / STEPS
    noise_level = SHIFT_FACTOR * fraction / (1.0 + (SHIFT_FACTOR - 1.0) * fraction)
    level = noise_level.reshape(1)

    left_z, right_z = seq_ring()
    left_y, right_y = y_ring()
    normed = normalize_turned(latent_in[0], gen_gain, places)
    pair = core_rows(
        [gen_qkv.reshape(gen_qkv.shape[0], -1), gen_out.reshape(gen_out.shape[0], -1)], core
    )
    normed, pair = lax.optimization_barrier((normed, pair))
    right_shard, left_shard = left_z(normed), right_z(normed)
    block = jnp.concatenate(ordered(x_half, pair, swap_half(pair)))
    block, score_qkv = lax.optimization_barrier((block, score_qkv))
    score_matrix = jnp.transpose(score_qkv[:, 0], (2, 1, 0, 3))
    right_block, left_block = left_y(block), right_y(block)
    right_shard, left_shard, score_matrix = lax.optimization_barrier(
        (right_shard, left_shard, score_matrix)
    )

    half = local_rows // 2
    rows = block.shape[0] // 2
    far_first, far_second, right_far, left_far, right_block, left_block = lax.optimization_barrier(
        (
            left_z(right_shard[:half]),
            right_z(left_shard[half:]),
            left_y(right_block[:rows]),
            right_y(left_block[rows:]),
            right_block,
            left_block,
        )
    )
    own_buffer = jnp.concatenate([block, right_block, right_far, left_far, left_block])
    other_buffer = swap_core(own_buffer)

    out_columns = own_buffer[:, 3 * head_width :]
    out_halves = out_columns.reshape(4, 2, -1, head_width)
    own_heads = swap_group(jnp.where(group == 0, out_halves[:, 1], out_halves[:, 0]))
    own_heads = own_heads.reshape(-1, head_width)

    moves = []
    for g in range(group_size):
        for f in range(fsdp_size):
            for s in range(seq_size):
                source = ((g ^ ((f // 2) % 2)) * fsdp_size + f) * seq_size + (s + f // 4) % seq_size
                moves.append((source, (g * fsdp_size + f) * seq_size + s))
    normed_parts = [normed, right_shard, far_first, far_second, left_shard]
    own_projected, own_mixed = generator_head(normed_parts, own_buffer, False)
    own_heads, own_mixed = lax.optimization_barrier((own_heads, own_mixed))
    other_heads = swap_core(own_heads)
    own_partner = swap_group(own_mixed)
    other_projected, other_mixed, normed_full = generator_head(
        normed_parts, other_buffer, True
    )
    other_mixed, buffer = lax.optimization_barrier((other_mixed, own_buffer))
    other_partner = swap_group(other_mixed)
    head_columns = lax.ppermute(
        out_columns_in_order(places, buffer, head_width), ("group", "fsdp", "seq"), moves
    )

    terms = update_terms(
        places,
        [own_mixed, own_partner, other_mixed, other_partner],
        [own_buffer, own_heads, other_buffer, other_heads],
        local_rows,
    )
    sums, head_columns = ring_sum(*terms[1:], seq_ring(), head_columns)
    polarity = (2 * group - 1).astype(F32)
    back_block = dot(head_columns, score_out[:, 0].reshape(model_width, -1), 0, 0)
    back_block = (polarity * back_block).astype(BF16)
    back_blocks = lax.all_gather(back_block, "fsdp", axis=0)
    *sums, _ = lax.optimization_barrier((*sums, back_block))
    own_made, own_noisy = generate_half(
        places, level, latent_in[0], noise[0], [terms[0], *sums]
    )
    other_made = swap_group(own_made)
    own_parts = ring_gather(own_noisy, seq_ring())
    generated, other_noisy = join_halves(places, level, own_made, other_made, noise[0])
    near_parts = [own_parts[0], own_parts[1], own_parts[4]]
    total, squares = project_own_half(places, near_parts, score_matrix, score_gain)
    right_other, left_other, total = lax.optimization_barrier(
        (left_z(other_noisy), right_z(other_noisy), total)
    )
    other_parts = [
        other_noisy,
        right_other,
        left_z(right_other[:half]),
        right_z(left_other[half:]),
        left_other,
    ]

    flipped, straight = score_terms(
        places, other_parts, own_parts[2:4], score_matrix, total, squares, back_blocks, score_gain
    )

    flipped_sum = ring_total(flipped[0], *ring_sum(*flipped[1:], seq_ring()))
    flipped_sum = swap_group(flipped_sum.astype(BF16))
    dmixed = ring_total(straight[0], *ring_sum(*straight[1:], seq_ring()))
    dmixed = (dmixed + flipped_sum.astype(F32)) * (-noise_level / float(fsdp_size))
    dmixed = dmixed.astype(BF16)

    dother = reverse_head(other_projected, dmixed[:, head_width:])
    sent = dot(normed_full, dother, 0, 0).astype(BF16)
    got = swap_core(sent)
    down = reverse_head(own_projected, dmixed[:, :head_width])
    pair = (dot(normed_full, down, 0, 0) + got.astype(F32)).reshape(4, model_width // 4, -1)
    rows = pair.shape[1] // 2
    summed = ring_total(
        pair[0],
        *ring_sum(
            jnp.concatenate([pair[2, :rows], pair[3, rows:]]).astype(BF16),
            jnp.concatenate([pair[2, rows:], pair[1, :rows]]).astype(BF16),
            pair[3, :rows],
            pair[1, rows:],
            y_ring(),
        ),
    )
    rows = rows // 2

    def rows_of(x, c):
        return lax.dynamic_slice_in_dim(summed, (2 * x + c) * rows, rows)

    over_x = swap_half(rows_of(1 - x_half, core).astype(BF16))
    over_core = swap_core(rows_of(x_half, 1 - core).astype(BF16))
    over_both = lax.ppermute(
        rows_of(1 - x_half, 1 - core).astype(BF16), "fsdp", [(i, i ^ 3) for i in range(fsdp_size)]
    )
    own_head = rows_of(x_half, core) + over_x.astype(F32)
    other_head = over_core.astype(F32) + over_both.astype(F32)
    gen_grad = jnp.concatenate(ordered(core, own_head, other_head), axis=1)
    return (generated[None], gen_grad.reshape(-1, gen_heads, 3, head_width))


def solution(mesh):
    in_specs = (
        P("fsdp", "seq", None),
        P("fsdp", "seq", None),
        P("fsdp"),
        P(),
        P("fsdp", ("group", "seq"), None, None),
        P("fsdp", ("group", "seq"), None),
        P("group", None),
        P(None, "group", "seq", None, None),
        P(None, "group", "seq", None),
    )
    out_specs = (P("fsdp", "seq", None), P("fsdp", ("group", "seq"), None, None))
    return jax.shard_map(local, mesh=mesh, in_specs=in_specs, out_specs=out_specs, check_vma=False)
```

```python
import functools

import jax
import jax.numpy as jnp
from jax import lax
from jax.experimental import pallas as pl
from jax.experimental.pallas import tpu as pltpu
from jax.sharding import PartitionSpec as P

STEPS = 1000
SHIFT_FACTOR = 3.0
EPSILON = 1e-06
LOG2_E = 1.4426950408889634
LN_2 = 0.6931471805599453
F32 = jnp.float32
BF16 = jnp.bfloat16
VMEM = pl.BlockSpec(memory_space=pltpu.VMEM)
SMEM = pl.BlockSpec(memory_space=pltpu.SMEM)
ANY = pl.BlockSpec(memory_space=pl.ANY)


def like(shape, dtype):
    return jax.ShapeDtypeStruct(shape, dtype)


def memory(mebibytes):
    return pltpu.CompilerParams(vmem_limit_bytes=mebibytes * 2**20)


def shift(axis, size, stride, step):
    length = lax.axis_size(axis)
    moves = []
    for i in range(length):
        place = (i // stride) % size
        moves.append((i, i + ((place + step) % size - place) * stride))
    return lambda piece: lax.ppermute(piece, axis, moves)


def seq_ring():
    size = lax.axis_size("seq")
    return shift("seq", size, 1, -1), shift("seq", size, 1, 1)


def y_ring():
    size = lax.axis_size("fsdp") // 4
    return shift("fsdp", size, 4, -1), shift("fsdp", size, 4, 1)


def swap_group(piece):
    return shift("group", 2, 1, 1)(piece)


def swap_core(piece):
    return shift("fsdp", 2, 1, 1)(piece)


def swap_half(piece):
    return shift("fsdp", 2, 2, 1)(piece)


def ring_gather(shard, ring):
    to_left, to_right = ring
    half = shard.shape[0] // 2
    right = to_left(shard)
    left = to_right(shard)
    return [shard, right, to_left(right[:half]), to_right(left[half:]), left]


def ring_sum(left_first, right_first, held_left, held_right, ring, beside=None):
    to_left, to_right = ring
    half = held_left.shape[0]
    from_right = to_left(left_first)
    from_left = to_right(right_first)
    if beside is not None:
        from_right, from_left, beside = lax.optimization_barrier((from_right, from_left, beside))
    from_right_last = to_left((held_left + from_right[:half].astype(F32)).astype(BF16))
    from_left_last = to_right((held_right + from_left[:half].astype(F32)).astype(BF16))
    sums = (from_left, from_right, from_right_last, from_left_last)
    return sums if beside is None else (sums, beside)


def ring_total(own, from_left, from_right, from_right_last, from_left_last):
    half = own.shape[0] // 2
    first = own[:half] + from_left[half:].astype(F32) + from_right_last.astype(F32)
    second = own[half:] + from_right[half:].astype(F32) + from_left_last.astype(F32)
    return jnp.concatenate([first, second])


def ordered(flag, own, other):
    first = jnp.where(flag == 0, own, other)
    second = jnp.where(flag == 0, other, own)
    return first, second


def core_rows(shards, core):
    keep, send = [], []
    for shard in shards:
        width = shard.shape[1] // 2
        low, high = shard[:, :width], shard[:, width:]
        keep.append(jnp.where(core == 0, low, high))
        send.append(jnp.where(core == 0, high, low))
    own = jnp.concatenate(keep, axis=1)
    other = swap_core(jnp.concatenate(send, axis=1))
    return jnp.concatenate(ordered(core, own, other))


def normalize_kernel(place_ref, values_ref, gain_ref, out_ref):
    blocks = 4
    width = values_ref.shape[1] // blocks
    values = values_ref[...].astype(F32)
    inverse_rms = lax.rsqrt(jnp.mean(values * values, axis=-1, keepdims=True) + EPSILON)
    for block in range(blocks):
        source = pl.multiple_of(lax.rem(place_ref[0] + block, blocks) * width, 128)
        part = values_ref[:, pl.ds(source, width)].astype(F32)
        out_ref[:, block * width : (block + 1) * width] = (
            part * inverse_rms * gain_ref[:, pl.ds(source, width)]
        ).astype(BF16)


def normalize_turned(values, gain_vector, places):
    return pl.pallas_call(
        normalize_kernel,
        out_shape=like(values.shape, BF16),
        in_specs=[SMEM, VMEM, VMEM],
        out_specs=VMEM,
        compiler_params=memory(16),
    )(places, values, gain_vector[None])


def unit_rows(values, scale):
    mean = jnp.mean(values * values, axis=-1, keepdims=True)
    return values * lax.rsqrt(mean + EPSILON) * scale


def dot(left, right, left_dim=1, right_dim=0):
    return lax.dot_general(
        left, right, (((left_dim,), (right_dim,)), ((), ())), preferred_element_type=F32
    )


def loop(count, body):
    lax.fori_loop(0, count, lambda index, carry: (body(index), carry)[1], 0)


def mix_scratch(tokens, width):
    return [
        pltpu.VMEM((tokens, width), BF16),
        pltpu.VMEM((width, tokens), BF16),
        pltpu.VMEM((tokens, width), BF16),
    ]


def mix_head(query, key, value, scratch, store):
    tokens, width = query.shape
    unit_query, turned_key, rounded = scratch
    unit_query[...] = unit_rows(query, LOG2_E * width**-0.5).astype(BF16)
    turned_key[...] = unit_rows(key, 1.0).T.astype(BF16)
    rounded[...] = value.astype(BF16)
    span = tokens // 3

    for first in range(0, tokens, span):
        weights = jnp.exp2(dot(unit_query[first : first + span, :], turned_key[...]))
        totals = jnp.sum(weights, axis=-1, keepdims=True)
        store(first, (dot(weights.astype(BF16), rounded[...]) / totals).astype(BF16))


def gather_parts(parts, target, sems):
    copies = []
    row = 0
    for index, part in enumerate(parts):
        rows = part.shape[0]
        copies.append(
            pltpu.make_async_copy(part, target.at[pl.ds(row, rows)], sems.at[index])
        )
        row += rows
    for copy in copies:
        copy.start()
    return copies


def head_kernel(count, *refs):
    parts, refs = refs[:count], refs[count:]
    buffer, projected, mixed, full, weight, query, key, value, sems, weight_sem = refs
    width = mixed.shape[1]
    copies = [
        pltpu.make_async_copy(buffer.at[:, pl.ds(0, 3 * width)], weight, weight_sem)
    ]
    copies[0].start()
    copies += gather_parts(parts, full, sems)
    for copy in copies:
        copy.wait()
    projected[...] = dot(full[...], weight[...])

    def store(first, rows):
        mixed[first : first + rows.shape[0], :] = rows

    mix_head(
        projected[:, :width],
        projected[:, width : 2 * width],
        projected[:, 2 * width :],
        (query, key, value),
        store,
    )


def generator_head(parts, buffer, keep):
    tokens = sum(part.shape[0] for part in parts)
    depth, width = buffer.shape[0], buffer.shape[1] // 4
    outs = [like((tokens, 3 * width), F32), like((tokens, width), BF16)]
    scratch = [pltpu.VMEM((depth, 3 * width), BF16)] + mix_scratch(tokens, width)
    scratch += [pltpu.SemaphoreType.DMA((len(parts),)), pltpu.SemaphoreType.DMA(())]
    if keep:
        outs.append(like((tokens, depth), BF16))
    else:
        scratch.insert(0, pltpu.VMEM((tokens, depth), BF16))
    return pl.pallas_call(
        functools.partial(head_kernel, len(parts)),
        out_shape=outs,
        in_specs=[ANY] * (len(parts) + 1),
        out_specs=[VMEM] * len(outs),
        scratch_shapes=scratch,
        compiler_params=memory(48),
    )(*parts, buffer)


def columns_kernel(places, buffer, out, sems):
    rows = out.shape[0] // 4
    first = buffer.shape[1] - out.shape[1]
    copies = []
    for block in range(4):
        place = pl.multiple_of(lax.rem(places[0] + block, 4) * rows, rows)
        copies.append(
            pltpu.make_async_copy(
                buffer.at[pl.ds(block * rows, rows), pl.ds(first, out.shape[1])],
                out.at[pl.ds(place, rows)],
                sems.at[block],
            )
        )
    for copy in copies:
        copy.start()
    for copy in copies:
        copy.wait()


def out_columns_in_order(places, buffer, width):
    return pl.pallas_call(
        columns_kernel,
        out_shape=like((buffer.shape[0], width), BF16),
        in_specs=[SMEM, ANY],
        out_specs=VMEM,
        scratch_shapes=[pltpu.SemaphoreType.DMA((4,))],
        compiler_params=memory(16),
    )(places, buffer)


def update_kernel(
    places, a_own, b_own, a_other, b_other, own_buffer, own_heads, other_buffer, other_heads,
    own, left, right, held_left, held_right, matrix, sems
):
    width = a_own.shape[1]
    size = own.shape[1] // 4
    copies = []
    for side, (buffer, heads) in enumerate(
        ((own_buffer, own_heads), (other_buffer, other_heads))
    ):
        for block in range(4):
            first = pl.multiple_of((2 * block + places[1]) * size, size)
            rows = pl.ds(block * size, size)
            for index, source in enumerate(
                (buffer.at[pl.ds(first, size), pl.ds(3 * width, width)], heads.at[rows])
            ):
                target = matrix.at[rows, pl.ds((2 * side + index) * width, width)]
                copies.append(
                    pltpu.make_async_copy(source, target, sems.at[side, 2 * block + index])
                )
    for copy in copies:
        copy.start()
    for copy in copies:
        copy.wait()
    mixed = jnp.concatenate([a_own[...], b_own[...], a_other[...], b_other[...]], axis=1)
    rows = own.shape[0]
    half = rows // 2

    def term(first, count):
        return dot(mixed[first : first + count], matrix[...], 1, 1)

    two = term(2 * rows, rows)
    left[:half, :] = two[:half].astype(BF16)
    right[:half, :] = two[half:].astype(BF16)
    three = term(3 * rows, rows)
    held_left[...] = three[:half]
    left[half:, :] = three[half:].astype(BF16)
    one = term(rows, rows)
    right[half:, :] = one[:half].astype(BF16)
    held_right[...] = one[half:]
    own[...] = term(0, rows)


def update_terms(places, mixed, weights, rows):
    width = weights[0].shape[0] // 2
    return pl.pallas_call(
        update_kernel,
        out_shape=[
            like((rows, width), F32),
            like((rows, width), BF16),
            like((rows, width), BF16),
            like((rows // 2, width), F32),
            like((rows // 2, width), F32),
        ],
        in_specs=[SMEM] + [VMEM] * 4 + [ANY] * 4,
        out_specs=[VMEM] * 5,
        scratch_shapes=[
            pltpu.VMEM((width, weights[0].shape[1]), BF16),
            pltpu.SemaphoreType.DMA((2, 8)),
        ],
        compiler_params=memory(24),
    )(places, *mixed, *weights)


def noisy_rows(level, generated, noise):
    return ((1.0 - level) * generated.astype(F32) + level * noise.astype(F32)).astype(BF16)


def generate_kernel(
    places, level, latent, noise, own, from_left, from_right, right_last, left_last, generated, noisy
):
    half = own.shape[0] // 2
    width = own.shape[1] // 4
    for block in range(4):
        columns = slice(block * width, (block + 1) * width)
        source = (lax.rem(places[0] + block, 4) * 2 + places[1]) * width
        source = pl.ds(pl.multiple_of(source, 128), width)
        for rows, near, last in (
            (slice(0, half), from_left, right_last),
            (slice(half, 2 * half), from_right, left_last),
        ):
            update = own[rows, columns] + near[half:, columns].astype(F32)
            update = update + last[:, columns].astype(F32)
            made = (latent[rows, source].astype(F32) + update).astype(BF16)
            generated[rows, columns] = made
            noisy[rows, columns] = noisy_rows(level[0], made, noise[rows, source])


def generate_half(places, level, latent, noise, terms):
    shape = terms[0].shape
    return pl.pallas_call(
        generate_kernel,
        out_shape=[like(shape, BF16), like(shape, BF16)],
        in_specs=[SMEM] * 2 + [VMEM] * 7,
        out_specs=[VMEM] * 2,
        compiler_params=memory(24),
    )(places, level, latent, noise, *terms)


def join_kernel(places, level, own, other, noise, generated, noisy):
    width = own.shape[1] // 4
    for block in range(4):
        columns = slice(block * width, (block + 1) * width)
        pair = lax.rem(places[0] + block, 4) * 2
        here = pl.ds(pl.multiple_of((pair + places[1]) * width, 128), width)
        there = pl.ds(pl.multiple_of((pair + 1 - places[1]) * width, 128), width)
        generated[:, here] = own[:, columns]
        made = other[:, columns]
        generated[:, there] = made
        noisy[:, columns] = noisy_rows(level[0], made, noise[:, there])


def join_halves(places, level, own, other, noise):
    return pl.pallas_call(
        join_kernel,
        out_shape=[like(noise.shape, BF16), like(own.shape, BF16)],
        in_specs=[SMEM] * 2 + [VMEM] * 3,
        out_specs=[VMEM] * 2,
        compiler_params=memory(24),
    )(places, level, own, other, noise)


def half_weight_copies(places, matrix, weight, sems, side, head):
    copies = []
    size = matrix.shape[2] // 8
    for block in range(4):
        first = (lax.rem(places[0] + block, 4) * 2 + side) * size
        rows = pl.ds(pl.multiple_of(first, size), size)
        copies.append(
            pltpu.make_async_copy(
                matrix.at[:, head, rows],
                weight.at[head, :, pl.ds(block * size, size)],
                sems.at[head, block],
            )
        )
    return copies


def head_weight(weight, head):
    return jnp.concatenate([weight[head, kind] for kind in range(weight.shape[1])], axis=1)


def scale_rows(places, side, full, gain, squares):
    size = gain.shape[1] // 8
    span = 96

    def scale(index):
        rows = pl.ds(pl.multiple_of(index * span, span), span)
        values = full[rows, :].astype(F32)
        sums = jnp.sum(values * values, axis=-1, keepdims=True)
        squares[rows, :] = jnp.broadcast_to(sums, (span, squares.shape[1]))
        for block in range(4):
            first = (lax.rem(places[0] + block, 4) * 2 + side) * size
            part = gain[:, pl.ds(pl.multiple_of(first, 128), size)]
            columns = slice(block * size, (block + 1) * size)
            full[rows, columns] = (values[:, columns] * part).astype(BF16)

    loop(full.shape[0] // span, scale)


def score_kernel(places, *refs):
    own_parts, parts, refs = refs[:5], refs[5:10], refs[10:]
    back_source, matrix, gain = refs[:3]
    outs = [refs[3:8], refs[8:13]]
    (
        own_full, full, own_weight, weight, back, mixed, own_squares, squares, inverse_rms,
        query, key, value, own_part_sems, part_sems, own_sems, sems, back_sem,
    ) = refs[13:]
    heads = sems.shape[0]
    width = weight.shape[1] * weight.shape[3]
    head_width = width // 3
    tokens = full.shape[0]
    step = tokens // 4
    half = tokens // 2

    def head_copies(head):
        return half_weight_copies(
            places, matrix, own_weight, own_sems, places[1], head
        ) + half_weight_copies(places, matrix, weight, sems, 1 - places[1], head)

    own_copies = gather_parts(own_parts, own_full, own_part_sems)
    copies = gather_parts(parts, full, part_sems)
    for head in range(heads):
        for copy in head_copies(head):
            copy.start()
    back_copy = pltpu.make_async_copy(back_source, back, back_sem)
    back_copy.start()
    for copy in own_copies:
        copy.wait()
    scale_rows(places, places[1], own_full, gain, own_squares)
    for copy in copies:
        copy.wait()
    scale_rows(places, 1 - places[1], full, gain, squares)
    mean = (own_squares[...] + squares[...]) / (2 * full.shape[1])
    inverse_rms[...] = lax.rsqrt(mean + EPSILON)

    def one_head(head):
        for copy in head_copies(head):
            copy.wait()
        projected = dot(own_full[...], head_weight(own_weight, head))
        projected = projected + dot(full[...], head_weight(weight, head))
        lanes = pl.ds(pl.multiple_of(head * head_width, 128), head_width)

        def store(first, rows):
            mixed[first : first + rows.shape[0], lanes] = rows

        mix_head(
            *[
                projected[:, kind * head_width : (kind + 1) * head_width] * inverse_rms[...]
                for kind in range(3)
            ],
            (query, key, value),
            store,
        )

    loop(heads, one_head)
    back_copy.wait()

    def back_part(block, flip):
        pair = (block * 2 + flip) * 2
        return jnp.concatenate([back[pair + places[2]], back[pair + 1 - places[2]]])

    for flip, (own, left, right, held_left, held_right) in zip((1, 0), outs):

        def term(block):
            start = block * step
            rows = mixed[...]
            if block:
                rows = jnp.concatenate([mixed[start:, :], mixed[:start, :]])
            return dot(rows, back_part(block, flip), 1, 1)

        two = term(2)
        left[:half, :] = two[:half].astype(BF16)
        right[:half, :] = two[half:].astype(BF16)
        three = term(3)
        held_left[...] = three[:half]
        left[half:, :] = three[half:].astype(BF16)
        one = term(1)
        right[half:, :] = one[:half].astype(BF16)
        held_right[...] = one[half:]
        own[...] = term(0)


def score_terms(places, own_parts, parts, matrix, back, gain):
    tokens = sum(part.shape[0] for part in parts)
    kinds, heads, _, head_width = matrix.shape
    depth = parts[0].shape[1]
    columns = 2 * back.shape[1]
    one = [
        like((tokens, columns), F32),
        like((tokens, columns), BF16),
        like((tokens, columns), BF16),
        like((tokens // 2, columns), F32),
        like((tokens // 2, columns), F32),
    ]
    outs = pl.pallas_call(
        score_kernel,
        out_shape=one + one,
        in_specs=[SMEM] + [ANY] * 12 + [VMEM],
        out_specs=[VMEM] * 10,
        scratch_shapes=[
            pltpu.VMEM((tokens, depth), BF16),
            pltpu.VMEM((tokens, depth), BF16),
            pltpu.VMEM((heads, kinds, depth, head_width), BF16),
            pltpu.VMEM((heads, kinds, depth, head_width), BF16),
            pltpu.VMEM(back.shape, BF16),
            pltpu.VMEM((tokens, heads * head_width), BF16),
            pltpu.VMEM((tokens, 128), F32),
            pltpu.VMEM((tokens, 128), F32),
            pltpu.VMEM((tokens, 128), F32),
            *mix_scratch(tokens, head_width),
            pltpu.SemaphoreType.DMA((5,)),
            pltpu.SemaphoreType.DMA((5,)),
            pltpu.SemaphoreType.DMA((heads, 4)),
            pltpu.SemaphoreType.DMA((heads, 4)),
            pltpu.SemaphoreType.DMA(()),
        ],
        compiler_params=memory(60),
    )(places, *own_parts, *parts, back, matrix, gain)
    return outs[:5], outs[5:]


def unit_reverse(values, gradient, scale):
    width = values.shape[-1]
    inverse = lax.rsqrt(jnp.mean(values * values, axis=-1, keepdims=True) + EPSILON)
    along = jnp.sum(gradient * values, axis=-1, keepdims=True) / width
    return scale * inverse * (gradient - values * (along * inverse * inverse))


def reverse_kernel(projected, gradient, out, key_total, value_total):
    tokens, width = gradient.shape
    query, key = projected[:, :width], projected[:, width : 2 * width]
    scale = width**-0.5
    unit_query = unit_rows(query, LOG2_E * scale).astype(BF16)
    unit_key = unit_rows(key, 1.0).astype(BF16)
    value = projected[:, 2 * width :]
    turned_key = unit_rows(key, 1.0).T.astype(BF16)
    turned_value = value.T.astype(BF16)
    value = value.astype(BF16)
    span = tokens // 3
    for first in range(0, tokens, span):
        rows = slice(first, first + span)
        weights = jnp.exp2(dot(unit_query[rows], turned_key))
        totals = jnp.sum(weights, axis=-1, keepdims=True)
        rounded = weights.astype(BF16)
        raw = dot(rounded, value)
        given = gradient[rows, :].astype(F32)
        draw = (given / totals).astype(BF16)
        dtotals = -jnp.sum(given * raw, axis=-1, keepdims=True) / (totals * totals)
        dweights = dot(draw, turned_value).astype(BF16).astype(F32) + dtotals
        dscores = (dweights * weights).astype(BF16)
        dquery = dot(dscores, unit_key).astype(BF16).astype(F32)
        out[rows, :width] = unit_reverse(query[rows], dquery, scale).astype(BF16)
        key_term = dot(dscores, unit_query[rows], 0, 0)
        value_term = dot(rounded, draw, 0, 0)
        if first == 0:
            key_total[...] = key_term
            value_total[...] = value_term
        else:
            key_total[...] += key_term
            value_total[...] += value_term
    dkey = (LN_2 * key_total[...]).astype(BF16).astype(F32)
    out[:, width : 2 * width] = unit_reverse(key, dkey, 1.0).astype(BF16)
    out[:, 2 * width :] = value_total[...].astype(BF16)


def reverse_head(projected, gradient):
    tokens, width = gradient.shape
    return pl.pallas_call(
        reverse_kernel,
        out_shape=like(projected.shape, BF16),
        in_specs=[VMEM] * 2,
        out_specs=VMEM,
        scratch_shapes=[pltpu.VMEM((tokens, width), F32), pltpu.VMEM((tokens, width), F32)],
        compiler_params=memory(24),
    )(projected, gradient)


def local(latent_in, noise, timestep, gen_gain, gen_qkv, gen_out, score_gain, score_qkv, score_out):
    place = lax.axis_index("fsdp")
    core, x_half, y_place = place % 2, (place // 2) % 2, place // 4
    group = lax.axis_index("group")
    fsdp_size = lax.axis_size("fsdp")
    seq_size = lax.axis_size("seq")
    group_size = lax.axis_size("group")
    head_width = gen_qkv.shape[-1]
    gen_heads = gen_qkv.shape[1]
    model_width = latent_in.shape[2]
    local_rows = latent_in.shape[1]
    places = jnp.stack([y_place, group, core]).astype(jnp.int32)

    fraction = (timestep[0].astype(F32) + 1.0) / STEPS
    noise_level = SHIFT_FACTOR * fraction / (1.0 + (SHIFT_FACTOR - 1.0) * fraction)
    level = noise_level.reshape(1)

    left_z, right_z = seq_ring()
    left_y, right_y = y_ring()
    normed = normalize_turned(latent_in[0], gen_gain, places)
    pair = core_rows(
        [gen_qkv.reshape(gen_qkv.shape[0], -1), gen_out.reshape(gen_out.shape[0], -1)], core
    )
    normed, pair = lax.optimization_barrier((normed, pair))
    right_shard, left_shard = left_z(normed), right_z(normed)
    block = jnp.concatenate(ordered(x_half, pair, swap_half(pair)))
    block, score_qkv = lax.optimization_barrier((block, score_qkv))
    score_matrix = jnp.transpose(score_qkv[:, 0], (2, 1, 0, 3))
    right_block, left_block = left_y(block), right_y(block)
    right_shard, left_shard, score_matrix = lax.optimization_barrier(
        (right_shard, left_shard, score_matrix)
    )

    half = local_rows // 2
    rows = block.shape[0] // 2
    far_first, far_second, right_far, left_far, right_block, left_block = lax.optimization_barrier(
        (
            left_z(right_shard[:half]),
            right_z(left_shard[half:]),
            left_y(right_block[:rows]),
            right_y(left_block[rows:]),
            right_block,
            left_block,
        )
    )
    own_buffer = jnp.concatenate([block, right_block, right_far, left_far, left_block])
    other_buffer = swap_core(own_buffer)

    out_columns = own_buffer[:, 3 * head_width :]
    out_halves = out_columns.reshape(4, 2, -1, head_width)
    own_heads = swap_group(jnp.where(group == 0, out_halves[:, 1], out_halves[:, 0]))
    own_heads = own_heads.reshape(-1, head_width)

    moves = []
    for g in range(group_size):
        for f in range(fsdp_size):
            for s in range(seq_size):
                source = ((g ^ ((f // 2) % 2)) * fsdp_size + f) * seq_size + (s + f // 4) % seq_size
                moves.append((source, (g * fsdp_size + f) * seq_size + s))
    normed_parts = [normed, right_shard, far_first, far_second, left_shard]
    own_projected, own_mixed = generator_head(normed_parts, own_buffer, False)
    own_heads, own_mixed = lax.optimization_barrier((own_heads, own_mixed))
    other_heads = swap_core(own_heads)
    own_partner = swap_group(own_mixed)
    other_projected, other_mixed, normed_full = generator_head(
        normed_parts, other_buffer, True
    )
    other_mixed, buffer = lax.optimization_barrier((other_mixed, own_buffer))
    other_partner = swap_group(other_mixed)
    head_columns = lax.ppermute(
        out_columns_in_order(places, buffer, head_width), ("group", "fsdp", "seq"), moves
    )

    terms = update_terms(
        places,
        [own_mixed, own_partner, other_mixed, other_partner],
        [own_buffer, own_heads, other_buffer, other_heads],
        local_rows,
    )
    sums, head_columns = ring_sum(*terms[1:], seq_ring(), head_columns)
    polarity = (2 * group - 1).astype(F32)
    back_block = dot(head_columns, score_out[:, 0].reshape(model_width, -1), 0, 0)
    back_block = (polarity * back_block).astype(BF16)
    back_blocks = lax.all_gather(back_block, "fsdp", axis=0)
    *sums, _ = lax.optimization_barrier((*sums, back_block))
    own_made, own_noisy = generate_half(
        places, level, latent_in[0], noise[0], [terms[0], *sums]
    )
    other_made = swap_group(own_made)
    own_parts = ring_gather(own_noisy, seq_ring())
    generated, other_noisy = join_halves(places, level, own_made, other_made, noise[0])
    other_parts = ring_gather(other_noisy, seq_ring())

    flipped, straight = score_terms(
        places, own_parts, other_parts, score_matrix, back_blocks, score_gain
    )

    flipped_sum = ring_total(flipped[0], *ring_sum(*flipped[1:], seq_ring()))
    flipped_sum = swap_group(flipped_sum.astype(BF16))
    dmixed = ring_total(straight[0], *ring_sum(*straight[1:], seq_ring()))
    dmixed = (dmixed + flipped_sum.astype(F32)) * (-noise_level / float(fsdp_size))
    dmixed = dmixed.astype(BF16)

    dother = reverse_head(other_projected, dmixed[:, head_width:])
    sent = dot(normed_full, dother, 0, 0).astype(BF16)
    got = swap_core(sent)
    down = reverse_head(own_projected, dmixed[:, :head_width])
    pair = (dot(normed_full, down, 0, 0) + got.astype(F32)).reshape(4, model_width // 4, -1)
    rows = pair.shape[1] // 2
    summed = ring_total(
        pair[0],
        *ring_sum(
            jnp.concatenate([pair[2, :rows], pair[3, rows:]]).astype(BF16),
            jnp.concatenate([pair[2, rows:], pair[1, :rows]]).astype(BF16),
            pair[3, :rows],
            pair[1, rows:],
            y_ring(),
        ),
    )
    rows = rows // 2

    def rows_of(x, c):
        return lax.dynamic_slice_in_dim(summed, (2 * x + c) * rows, rows)

    over_x = swap_half(rows_of(1 - x_half, core).astype(BF16))
    over_core = swap_core(rows_of(x_half, 1 - core).astype(BF16))
    over_both = lax.ppermute(
        rows_of(1 - x_half, 1 - core).astype(BF16), "fsdp", [(i, i ^ 3) for i in range(fsdp_size)]
    )
    own_head = rows_of(x_half, core) + over_x.astype(F32)
    other_head = over_core.astype(F32) + over_both.astype(F32)
    gen_grad = jnp.concatenate(ordered(core, own_head, other_head), axis=1)
    return (generated[None], gen_grad.reshape(-1, gen_heads, 3, head_width))


def solution(mesh):
    in_specs = (
        P("fsdp", "seq", None),
        P("fsdp", "seq", None),
        P("fsdp"),
        P(),
        P("fsdp", ("group", "seq"), None, None),
        P("fsdp", ("group", "seq"), None),
        P("group", None),
        P(None, "group", "seq", None, None),
        P(None, "group", "seq", None),
    )
    out_specs = (P("fsdp", "seq", None), P("fsdp", ("group", "seq"), None, None))
    return jax.shard_map(local, mesh=mesh, in_specs=in_specs, out_specs=out_specs, check_vma=False)
```

```python
import functools

import jax
import jax.numpy as jnp
from jax import lax
from jax.experimental import pallas as pl
from jax.experimental.pallas import tpu as pltpu
from jax.sharding import PartitionSpec as P

STEPS = 1000
SHIFT_FACTOR = 3.0
EPSILON = 1e-06
LOG2_E = 1.4426950408889634
LN_2 = 0.6931471805599453
F32 = jnp.float32
BF16 = jnp.bfloat16
VMEM = pl.BlockSpec(memory_space=pltpu.VMEM)
SMEM = pl.BlockSpec(memory_space=pltpu.SMEM)
ANY = pl.BlockSpec(memory_space=pl.ANY)


def like(shape, dtype):
    return jax.ShapeDtypeStruct(shape, dtype)


def memory(mebibytes):
    return pltpu.CompilerParams(vmem_limit_bytes=mebibytes * 2**20)


def shift(axis, size, stride, step):
    length = lax.axis_size(axis)
    moves = []
    for i in range(length):
        place = (i // stride) % size
        moves.append((i, i + ((place + step) % size - place) * stride))
    return lambda piece: lax.ppermute(piece, axis, moves)


def seq_ring():
    size = lax.axis_size("seq")
    return shift("seq", size, 1, -1), shift("seq", size, 1, 1)


def y_ring():
    size = lax.axis_size("fsdp") // 4
    return shift("fsdp", size, 4, -1), shift("fsdp", size, 4, 1)


def swap_group(piece):
    return shift("group", 2, 1, 1)(piece)


def swap_core(piece):
    return shift("fsdp", 2, 1, 1)(piece)


def swap_half(piece):
    return shift("fsdp", 2, 2, 1)(piece)


def ring_gather(shard, ring):
    to_left, to_right = ring
    half = shard.shape[0] // 2
    right = to_left(shard)
    left = to_right(shard)
    return [shard, right, to_left(right[:half]), to_right(left[half:]), left]


def ring_sum(left_first, right_first, held_left, held_right, ring, beside=None):
    to_left, to_right = ring
    half = held_left.shape[0]
    from_right = to_left(left_first)
    from_left = to_right(right_first)
    if beside is not None:
        from_right, from_left, beside = lax.optimization_barrier((from_right, from_left, beside))
    from_right_last = to_left((held_left + from_right[:half].astype(F32)).astype(BF16))
    from_left_last = to_right((held_right + from_left[:half].astype(F32)).astype(BF16))
    sums = (from_left, from_right, from_right_last, from_left_last)
    return sums if beside is None else (sums, beside)


def ring_total(own, from_left, from_right, from_right_last, from_left_last):
    half = own.shape[0] // 2
    first = own[:half] + from_left[half:].astype(F32) + from_right_last.astype(F32)
    second = own[half:] + from_right[half:].astype(F32) + from_left_last.astype(F32)
    return jnp.concatenate([first, second])


def ordered(flag, own, other):
    first = jnp.where(flag == 0, own, other)
    second = jnp.where(flag == 0, other, own)
    return first, second


def core_rows(shards, core):
    keep, send = [], []
    for shard in shards:
        width = shard.shape[1] // 2
        low, high = shard[:, :width], shard[:, width:]
        keep.append(jnp.where(core == 0, low, high))
        send.append(jnp.where(core == 0, high, low))
    own = jnp.concatenate(keep, axis=1)
    other = swap_core(jnp.concatenate(send, axis=1))
    return jnp.concatenate(ordered(core, own, other))


def normalize_kernel(place_ref, values_ref, gain_ref, out_ref):
    blocks = 4
    width = values_ref.shape[1] // blocks
    values = values_ref[...].astype(F32)
    inverse_rms = lax.rsqrt(jnp.mean(values * values, axis=-1, keepdims=True) + EPSILON)
    for block in range(blocks):
        source = pl.multiple_of(lax.rem(place_ref[0] + block, blocks) * width, 128)
        part = values_ref[:, pl.ds(source, width)].astype(F32)
        out_ref[:, block * width : (block + 1) * width] = (
            part * inverse_rms * gain_ref[:, pl.ds(source, width)]
        ).astype(BF16)


def normalize_turned(values, gain_vector, places):
    return pl.pallas_call(
        normalize_kernel,
        out_shape=like(values.shape, BF16),
        in_specs=[SMEM, VMEM, VMEM],
        out_specs=VMEM,
        compiler_params=memory(16),
    )(places, values, gain_vector[None])


def unit_rows(values, scale):
    mean = jnp.mean(values * values, axis=-1, keepdims=True)
    return values * lax.rsqrt(mean + EPSILON) * scale


def dot(left, right, left_dim=1, right_dim=0):
    return lax.dot_general(
        left, right, (((left_dim,), (right_dim,)), ((), ())), preferred_element_type=F32
    )


def loop(count, body):
    lax.fori_loop(0, count, lambda index, carry: (body(index), carry)[1], 0)


def mix_scratch(tokens, width):
    return [
        pltpu.VMEM((tokens, width), BF16),
        pltpu.VMEM((width, tokens), BF16),
        pltpu.VMEM((tokens, width), BF16),
    ]


def mix_head(query, key, value, scratch, store):
    tokens, width = query.shape
    unit_query, turned_key, rounded = scratch
    unit_query[...] = unit_rows(query, LOG2_E * width**-0.5).astype(BF16)
    turned_key[...] = unit_rows(key, 1.0).T.astype(BF16)
    rounded[...] = value.astype(BF16)
    span = tokens // 3

    for first in range(0, tokens, span):
        weights = jnp.exp2(dot(unit_query[first : first + span, :], turned_key[...]))
        totals = jnp.sum(weights, axis=-1, keepdims=True)
        store(first, (dot(weights.astype(BF16), rounded[...]) / totals).astype(BF16))


def gather_parts(parts, target, sems):
    copies = []
    row = 0
    for index, part in enumerate(parts):
        rows = part.shape[0]
        copies.append(
            pltpu.make_async_copy(part, target.at[pl.ds(row, rows)], sems.at[index])
        )
        row += rows
    for copy in copies:
        copy.start()
    return copies


def head_kernel(count, *refs):
    parts, refs = refs[:count], refs[count:]
    buffer, projected, mixed, full, weight, query, key, value, sems, weight_sem = refs
    width = mixed.shape[1]
    copies = [
        pltpu.make_async_copy(buffer.at[:, pl.ds(0, 3 * width)], weight, weight_sem)
    ]
    copies[0].start()
    copies += gather_parts(parts, full, sems)
    for copy in copies:
        copy.wait()
    projected[...] = dot(full[...], weight[...])

    def store(first, rows):
        mixed[first : first + rows.shape[0], :] = rows

    mix_head(
        projected[:, :width],
        projected[:, width : 2 * width],
        projected[:, 2 * width :],
        (query, key, value),
        store,
    )


def generator_head(parts, buffer, keep):
    tokens = sum(part.shape[0] for part in parts)
    depth, width = buffer.shape[0], buffer.shape[1] // 4
    outs = [like((tokens, 3 * width), F32), like((tokens, width), BF16)]
    scratch = [pltpu.VMEM((depth, 3 * width), BF16)] + mix_scratch(tokens, width)
    scratch += [pltpu.SemaphoreType.DMA((len(parts),)), pltpu.SemaphoreType.DMA(())]
    if keep:
        outs.append(like((tokens, depth), BF16))
    else:
        scratch.insert(0, pltpu.VMEM((tokens, depth), BF16))
    return pl.pallas_call(
        functools.partial(head_kernel, len(parts)),
        out_shape=outs,
        in_specs=[ANY] * (len(parts) + 1),
        out_specs=[VMEM] * len(outs),
        scratch_shapes=scratch,
        compiler_params=memory(48),
    )(*parts, buffer)


def columns_kernel(places, buffer, out, sems):
    rows = out.shape[0] // 4
    first = buffer.shape[1] - out.shape[1]
    copies = []
    for block in range(4):
        place = pl.multiple_of(lax.rem(places[0] + block, 4) * rows, rows)
        copies.append(
            pltpu.make_async_copy(
                buffer.at[pl.ds(block * rows, rows), pl.ds(first, out.shape[1])],
                out.at[pl.ds(place, rows)],
                sems.at[block],
            )
        )
    for copy in copies:
        copy.start()
    for copy in copies:
        copy.wait()


def out_columns_in_order(places, buffer, width):
    return pl.pallas_call(
        columns_kernel,
        out_shape=like((buffer.shape[0], width), BF16),
        in_specs=[SMEM, ANY],
        out_specs=VMEM,
        scratch_shapes=[pltpu.SemaphoreType.DMA((4,))],
        compiler_params=memory(16),
    )(places, buffer)


def update_kernel(
    places, a_own, b_own, a_other, b_other, own_buffer, own_heads, other_buffer, other_heads,
    own, left, right, held_left, held_right, matrix, sems
):
    width = a_own.shape[1]
    size = own.shape[1] // 4
    copies = []
    for side, (buffer, heads) in enumerate(
        ((own_buffer, own_heads), (other_buffer, other_heads))
    ):
        for block in range(4):
            first = pl.multiple_of((2 * block + places[1]) * size, size)
            rows = pl.ds(block * size, size)
            for index, source in enumerate(
                (buffer.at[pl.ds(first, size), pl.ds(3 * width, width)], heads.at[rows])
            ):
                target = matrix.at[rows, pl.ds((2 * side + index) * width, width)]
                copies.append(
                    pltpu.make_async_copy(source, target, sems.at[side, 2 * block + index])
                )
    for copy in copies:
        copy.start()
    for copy in copies:
        copy.wait()
    mixed = jnp.concatenate([a_own[...], b_own[...], a_other[...], b_other[...]], axis=1)
    rows = own.shape[0]
    half = rows // 2

    def term(first, count):
        return dot(mixed[first : first + count], matrix[...], 1, 1)

    two = term(2 * rows, rows)
    left[:half, :] = two[:half].astype(BF16)
    right[:half, :] = two[half:].astype(BF16)
    three = term(3 * rows, rows)
    held_left[...] = three[:half]
    left[half:, :] = three[half:].astype(BF16)
    one = term(rows, rows)
    right[half:, :] = one[:half].astype(BF16)
    held_right[...] = one[half:]
    own[...] = term(0, rows)


def update_terms(places, mixed, weights, rows):
    width = weights[0].shape[0] // 2
    return pl.pallas_call(
        update_kernel,
        out_shape=[
            like((rows, width), F32),
            like((rows, width), BF16),
            like((rows, width), BF16),
            like((rows // 2, width), F32),
            like((rows // 2, width), F32),
        ],
        in_specs=[SMEM] + [VMEM] * 4 + [ANY] * 4,
        out_specs=[VMEM] * 5,
        scratch_shapes=[
            pltpu.VMEM((width, weights[0].shape[1]), BF16),
            pltpu.SemaphoreType.DMA((2, 8)),
        ],
        compiler_params=memory(24),
    )(places, *mixed, *weights)


def noisy_rows(level, generated, noise):
    return ((1.0 - level) * generated.astype(F32) + level * noise.astype(F32)).astype(BF16)


def generate_kernel(
    places, level, latent, noise, own, from_left, from_right, right_last, left_last, generated, noisy
):
    half = own.shape[0] // 2
    width = own.shape[1] // 4
    for block in range(4):
        columns = slice(block * width, (block + 1) * width)
        source = (lax.rem(places[0] + block, 4) * 2 + places[1]) * width
        source = pl.ds(pl.multiple_of(source, 128), width)
        for rows, near, last in (
            (slice(0, half), from_left, right_last),
            (slice(half, 2 * half), from_right, left_last),
        ):
            update = own[rows, columns] + near[half:, columns].astype(F32)
            update = update + last[:, columns].astype(F32)
            made = (latent[rows, source].astype(F32) + update).astype(BF16)
            generated[rows, columns] = made
            noisy[rows, columns] = noisy_rows(level[0], made, noise[rows, source])


def generate_half(places, level, latent, noise, terms):
    shape = terms[0].shape
    return pl.pallas_call(
        generate_kernel,
        out_shape=[like(shape, BF16), like(shape, BF16)],
        in_specs=[SMEM] * 2 + [VMEM] * 7,
        out_specs=[VMEM] * 2,
        compiler_params=memory(24),
    )(places, level, latent, noise, *terms)


def join_kernel(places, level, own, other, noise, generated, noisy):
    width = own.shape[1] // 4
    for block in range(4):
        columns = slice(block * width, (block + 1) * width)
        pair = lax.rem(places[0] + block, 4) * 2
        here = pl.ds(pl.multiple_of((pair + places[1]) * width, 128), width)
        there = pl.ds(pl.multiple_of((pair + 1 - places[1]) * width, 128), width)
        generated[:, here] = own[:, columns]
        made = other[:, columns]
        generated[:, there] = made
        noisy[:, columns] = noisy_rows(level[0], made, noise[:, there])


def join_halves(places, level, own, other, noise):
    return pl.pallas_call(
        join_kernel,
        out_shape=[like(noise.shape, BF16), like(own.shape, BF16)],
        in_specs=[SMEM] * 2 + [VMEM] * 3,
        out_specs=[VMEM] * 2,
        compiler_params=memory(24),
    )(places, level, own, other, noise)


def half_weight_copies(places, matrix, weight, sems, side, head):
    copies = []
    size = matrix.shape[2] // 8
    for block in range(4):
        first = (lax.rem(places[0] + block, 4) * 2 + side) * size
        rows = pl.ds(pl.multiple_of(first, size), size)
        copies.append(
            pltpu.make_async_copy(
                matrix.at[:, head, rows],
                weight.at[head, :, pl.ds(block * size, size)],
                sems.at[head, block],
            )
        )
    return copies


def head_weight(weight, head):
    return jnp.concatenate([weight[head, kind] for kind in range(weight.shape[1])], axis=1)


def scale_rows(places, side, full, gain, squares):
    size = gain.shape[1] // 8
    span = 96

    def scale(index):
        rows = pl.ds(pl.multiple_of(index * span, span), span)
        values = full[rows, :].astype(F32)
        sums = jnp.sum(values * values, axis=-1, keepdims=True)
        squares[rows, :] = jnp.broadcast_to(sums, (span, squares.shape[1]))
        for block in range(4):
            first = (lax.rem(places[0] + block, 4) * 2 + side) * size
            part = gain[:, pl.ds(pl.multiple_of(first, 128), size)]
            columns = slice(block * size, (block + 1) * size)
            full[rows, columns] = (values[:, columns] * part).astype(BF16)

    loop(full.shape[0] // span, scale)


def score_kernel(places, *refs):
    own_parts, parts, refs = refs[:5], refs[5:10], refs[10:]
    back_source, matrix, gain = refs[:3]
    outs = [refs[3:8], refs[8:13]]
    (
        own_full, full, own_weight, weight, back, mixed, own_squares, squares, inverse_rms,
        query, key, value, own_part_sems, part_sems, own_sems, sems, back_sem,
    ) = refs[13:]
    heads = sems.shape[0]
    width = weight.shape[1] * weight.shape[3]
    head_width = width // 3
    tokens = full.shape[0]
    step = tokens // 4
    half = tokens // 2

    def head_copies(head):
        return half_weight_copies(
            places, matrix, own_weight, own_sems, places[1], head
        ) + half_weight_copies(places, matrix, weight, sems, 1 - places[1], head)

    own_copies = gather_parts(own_parts, own_full, own_part_sems)
    copies = gather_parts(parts, full, part_sems)
    for head in range(heads):
        for copy in head_copies(head):
            copy.start()
    back_copy = pltpu.make_async_copy(back_source, back, back_sem)
    back_copy.start()
    for copy in own_copies:
        copy.wait()
    scale_rows(places, places[1], own_full, gain, own_squares)
    for copy in copies:
        copy.wait()
    scale_rows(places, 1 - places[1], full, gain, squares)
    mean = (own_squares[...] + squares[...]) / (2 * full.shape[1])
    inverse_rms[...] = lax.rsqrt(mean + EPSILON)

    def one_head(head):
        for copy in head_copies(head):
            copy.wait()
        projected = dot(own_full[...], head_weight(own_weight, head))
        projected = projected + dot(full[...], head_weight(weight, head))
        lanes = pl.ds(pl.multiple_of(head * head_width, 128), head_width)

        def store(first, rows):
            mixed[first : first + rows.shape[0], lanes] = rows

        mix_head(
            *[
                projected[:, kind * head_width : (kind + 1) * head_width] * inverse_rms[...]
                for kind in range(3)
            ],
            (query, key, value),
            store,
        )

    loop(heads, one_head)
    back_copy.wait()

    def back_part(block, flip):
        pair = (block * 2 + flip) * 2
        return jnp.concatenate([back[pair + places[2]], back[pair + 1 - places[2]]])

    for flip, (own, left, right, held_left, held_right) in zip((1, 0), outs):

        def term(block):
            start = block * step
            rows = mixed[...]
            if block:
                rows = jnp.concatenate([mixed[start:, :], mixed[:start, :]])
            return dot(rows, back_part(block, flip), 1, 1)

        two = term(2)
        left[:half, :] = two[:half].astype(BF16)
        right[:half, :] = two[half:].astype(BF16)
        three = term(3)
        held_left[...] = three[:half]
        left[half:, :] = three[half:].astype(BF16)
        one = term(1)
        right[half:, :] = one[:half].astype(BF16)
        held_right[...] = one[half:]
        own[...] = term(0)


def score_terms(places, own_parts, parts, matrix, back, gain):
    tokens = sum(part.shape[0] for part in parts)
    kinds, heads, _, head_width = matrix.shape
    depth = parts[0].shape[1]
    columns = 2 * back.shape[1]
    one = [
        like((tokens, columns), F32),
        like((tokens, columns), BF16),
        like((tokens, columns), BF16),
        like((tokens // 2, columns), F32),
        like((tokens // 2, columns), F32),
    ]
    outs = pl.pallas_call(
        score_kernel,
        out_shape=one + one,
        in_specs=[SMEM] + [ANY] * 12 + [VMEM],
        out_specs=[VMEM] * 10,
        scratch_shapes=[
            pltpu.VMEM((tokens, depth), BF16),
            pltpu.VMEM((tokens, depth), BF16),
            pltpu.VMEM((heads, kinds, depth, head_width), BF16),
            pltpu.VMEM((heads, kinds, depth, head_width), BF16),
            pltpu.VMEM(back.shape, BF16),
            pltpu.VMEM((tokens, heads * head_width), BF16),
            pltpu.VMEM((tokens, 128), F32),
            pltpu.VMEM((tokens, 128), F32),
            pltpu.VMEM((tokens, 128), F32),
            *mix_scratch(tokens, head_width),
            pltpu.SemaphoreType.DMA((5,)),
            pltpu.SemaphoreType.DMA((5,)),
            pltpu.SemaphoreType.DMA((heads, 4)),
            pltpu.SemaphoreType.DMA((heads, 4)),
            pltpu.SemaphoreType.DMA(()),
        ],
        compiler_params=memory(44),
    )(places, *own_parts, *parts, back, matrix, gain)
    return outs[:5], outs[5:]


def unit_reverse(values, gradient, scale):
    width = values.shape[-1]
    inverse = lax.rsqrt(jnp.mean(values * values, axis=-1, keepdims=True) + EPSILON)
    along = jnp.sum(gradient * values, axis=-1, keepdims=True) / width
    return scale * inverse * (gradient - values * (along * inverse * inverse))


def reverse_kernel(projected, gradient, out, key_total, value_total):
    tokens, width = gradient.shape
    query, key = projected[:, :width], projected[:, width : 2 * width]
    scale = width**-0.5
    unit_query = unit_rows(query, LOG2_E * scale).astype(BF16)
    unit_key = unit_rows(key, 1.0).astype(BF16)
    value = projected[:, 2 * width :]
    turned_key = unit_rows(key, 1.0).T.astype(BF16)
    turned_value = value.T.astype(BF16)
    value = value.astype(BF16)
    span = tokens // 3
    for first in range(0, tokens, span):
        rows = slice(first, first + span)
        weights = jnp.exp2(dot(unit_query[rows], turned_key))
        totals = jnp.sum(weights, axis=-1, keepdims=True)
        rounded = weights.astype(BF16)
        raw = dot(rounded, value)
        given = gradient[rows, :].astype(F32)
        draw = (given / totals).astype(BF16)
        dtotals = -jnp.sum(given * raw, axis=-1, keepdims=True) / (totals * totals)
        dweights = dot(draw, turned_value).astype(BF16).astype(F32) + dtotals
        dscores = (dweights * weights).astype(BF16)
        dquery = dot(dscores, unit_key).astype(BF16).astype(F32)
        out[rows, :width] = unit_reverse(query[rows], dquery, scale).astype(BF16)
        key_term = dot(dscores, unit_query[rows], 0, 0)
        value_term = dot(rounded, draw, 0, 0)
        if first == 0:
            key_total[...] = key_term
            value_total[...] = value_term
        else:
            key_total[...] += key_term
            value_total[...] += value_term
    dkey = (LN_2 * key_total[...]).astype(BF16).astype(F32)
    out[:, width : 2 * width] = unit_reverse(key, dkey, 1.0).astype(BF16)
    out[:, 2 * width :] = value_total[...].astype(BF16)


def reverse_head(projected, gradient):
    tokens, width = gradient.shape
    return pl.pallas_call(
        reverse_kernel,
        out_shape=like(projected.shape, BF16),
        in_specs=[VMEM] * 2,
        out_specs=VMEM,
        scratch_shapes=[pltpu.VMEM((tokens, width), F32), pltpu.VMEM((tokens, width), F32)],
        compiler_params=memory(24),
    )(projected, gradient)


def local(latent_in, noise, timestep, gen_gain, gen_qkv, gen_out, score_gain, score_qkv, score_out):
    place = lax.axis_index("fsdp")
    core, x_half, y_place = place % 2, (place // 2) % 2, place // 4
    group = lax.axis_index("group")
    fsdp_size = lax.axis_size("fsdp")
    seq_size = lax.axis_size("seq")
    group_size = lax.axis_size("group")
    head_width = gen_qkv.shape[-1]
    gen_heads = gen_qkv.shape[1]
    model_width = latent_in.shape[2]
    local_rows = latent_in.shape[1]
    places = jnp.stack([y_place, group, core]).astype(jnp.int32)

    fraction = (timestep[0].astype(F32) + 1.0) / STEPS
    noise_level = SHIFT_FACTOR * fraction / (1.0 + (SHIFT_FACTOR - 1.0) * fraction)
    level = noise_level.reshape(1)

    left_z, right_z = seq_ring()
    left_y, right_y = y_ring()
    normed = normalize_turned(latent_in[0], gen_gain, places)
    pair = core_rows(
        [gen_qkv.reshape(gen_qkv.shape[0], -1), gen_out.reshape(gen_out.shape[0], -1)], core
    )
    normed, pair = lax.optimization_barrier((normed, pair))
    right_shard, left_shard = left_z(normed), right_z(normed)
    block = jnp.concatenate(ordered(x_half, pair, swap_half(pair)))
    block, score_qkv = lax.optimization_barrier((block, score_qkv))
    score_matrix = jnp.transpose(score_qkv[:, 0], (2, 1, 0, 3))
    right_block, left_block = left_y(block), right_y(block)
    right_shard, left_shard, score_matrix = lax.optimization_barrier(
        (right_shard, left_shard, score_matrix)
    )

    half = local_rows // 2
    rows = block.shape[0] // 2
    far_first, far_second, right_far, left_far, right_block, left_block = lax.optimization_barrier(
        (
            left_z(right_shard[:half]),
            right_z(left_shard[half:]),
            left_y(right_block[:rows]),
            right_y(left_block[rows:]),
            right_block,
            left_block,
        )
    )
    own_buffer = jnp.concatenate([block, right_block, right_far, left_far, left_block])
    other_buffer = swap_core(own_buffer)

    out_columns = own_buffer[:, 3 * head_width :]
    out_halves = out_columns.reshape(4, 2, -1, head_width)
    own_heads = swap_group(jnp.where(group == 0, out_halves[:, 1], out_halves[:, 0]))
    own_heads = own_heads.reshape(-1, head_width)

    moves = []
    for g in range(group_size):
        for f in range(fsdp_size):
            for s in range(seq_size):
                source = ((g ^ ((f // 2) % 2)) * fsdp_size + f) * seq_size + (s + f // 4) % seq_size
                moves.append((source, (g * fsdp_size + f) * seq_size + s))
    normed_parts = [normed, right_shard, far_first, far_second, left_shard]
    own_projected, own_mixed = generator_head(normed_parts, own_buffer, False)
    own_heads, own_mixed = lax.optimization_barrier((own_heads, own_mixed))
    other_heads = swap_core(own_heads)
    own_partner = swap_group(own_mixed)
    other_projected, other_mixed, normed_full = generator_head(
        normed_parts, other_buffer, True
    )
    other_mixed, buffer = lax.optimization_barrier((other_mixed, own_buffer))
    other_partner = swap_group(other_mixed)
    head_columns = lax.ppermute(
        out_columns_in_order(places, buffer, head_width), ("group", "fsdp", "seq"), moves
    )

    terms = update_terms(
        places,
        [own_mixed, own_partner, other_mixed, other_partner],
        [own_buffer, own_heads, other_buffer, other_heads],
        local_rows,
    )
    sums, head_columns = ring_sum(*terms[1:], seq_ring(), head_columns)
    polarity = (2 * group - 1).astype(F32)
    back_block = dot(head_columns, score_out[:, 0].reshape(model_width, -1), 0, 0)
    back_block = (polarity * back_block).astype(BF16)
    back_blocks = lax.all_gather(back_block, "fsdp", axis=0)
    *sums, _ = lax.optimization_barrier((*sums, back_block))
    own_made, own_noisy = generate_half(
        places, level, latent_in[0], noise[0], [terms[0], *sums]
    )
    other_made = swap_group(own_made)
    own_parts = ring_gather(own_noisy, seq_ring())
    generated, other_noisy = join_halves(places, level, own_made, other_made, noise[0])
    other_parts = ring_gather(other_noisy, seq_ring())

    flipped, straight = score_terms(
        places, own_parts, other_parts, score_matrix, back_blocks, score_gain
    )

    flipped_sum = ring_total(flipped[0], *ring_sum(*flipped[1:], seq_ring()))
    flipped_sum = swap_group(flipped_sum.astype(BF16))
    dmixed = ring_total(straight[0], *ring_sum(*straight[1:], seq_ring()))
    dmixed = (dmixed + flipped_sum.astype(F32)) * (-noise_level / float(fsdp_size))
    dmixed = dmixed.astype(BF16)

    dother = reverse_head(other_projected, dmixed[:, head_width:])
    sent = dot(normed_full, dother, 0, 0).astype(BF16)
    got = swap_core(sent)
    down = reverse_head(own_projected, dmixed[:, :head_width])
    pair = (dot(normed_full, down, 0, 0) + got.astype(F32)).reshape(4, model_width // 4, -1)
    rows = pair.shape[1] // 2
    summed = ring_total(
        pair[0],
        *ring_sum(
            jnp.concatenate([pair[2, :rows], pair[3, rows:]]).astype(BF16),
            jnp.concatenate([pair[2, rows:], pair[1, :rows]]).astype(BF16),
            pair[3, :rows],
            pair[1, rows:],
            y_ring(),
        ),
    )
    rows = rows // 2

    def rows_of(x, c):
        return lax.dynamic_slice_in_dim(summed, (2 * x + c) * rows, rows)

    over_x = swap_half(rows_of(1 - x_half, core).astype(BF16))
    over_core = swap_core(rows_of(x_half, 1 - core).astype(BF16))
    over_both = lax.ppermute(
        rows_of(1 - x_half, 1 - core).astype(BF16), "fsdp", [(i, i ^ 3) for i in range(fsdp_size)]
    )
    own_head = rows_of(x_half, core) + over_x.astype(F32)
    other_head = over_core.astype(F32) + over_both.astype(F32)
    gen_grad = jnp.concatenate(ordered(core, own_head, other_head), axis=1)
    return (generated[None], gen_grad.reshape(-1, gen_heads, 3, head_width))


def solution(mesh):
    in_specs = (
        P("fsdp", "seq", None),
        P("fsdp", "seq", None),
        P("fsdp"),
        P(),
        P("fsdp", ("group", "seq"), None, None),
        P("fsdp", ("group", "seq"), None),
        P("group", None),
        P(None, "group", "seq", None, None),
        P(None, "group", "seq", None),
    )
    out_specs = (P("fsdp", "seq", None), P("fsdp", ("group", "seq"), None, None))
    return jax.shard_map(local, mesh=mesh, in_specs=in_specs, out_specs=out_specs, check_vma=False)
```

```python
import functools

import jax
import jax.numpy as jnp
from jax import lax
from jax.experimental import pallas as pl
from jax.experimental.pallas import tpu as pltpu
from jax.sharding import PartitionSpec as P

STEPS = 1000
SHIFT_FACTOR = 3.0
EPSILON = 1e-06
LOG2_E = 1.4426950408889634
LN_2 = 0.6931471805599453
F32 = jnp.float32
BF16 = jnp.bfloat16
VMEM = pl.BlockSpec(memory_space=pltpu.VMEM)
SMEM = pl.BlockSpec(memory_space=pltpu.SMEM)
ANY = pl.BlockSpec(memory_space=pl.ANY)


def like(shape, dtype):
    return jax.ShapeDtypeStruct(shape, dtype)


def memory(mebibytes):
    return pltpu.CompilerParams(vmem_limit_bytes=mebibytes * 2**20)


def shift(axis, size, stride, step):
    length = lax.axis_size(axis)
    moves = []
    for i in range(length):
        place = (i // stride) % size
        moves.append((i, i + ((place + step) % size - place) * stride))
    return lambda piece: lax.ppermute(piece, axis, moves)


def seq_ring():
    size = lax.axis_size("seq")
    return shift("seq", size, 1, -1), shift("seq", size, 1, 1)


def y_ring():
    size = lax.axis_size("fsdp") // 4
    return shift("fsdp", size, 4, -1), shift("fsdp", size, 4, 1)


def swap_group(piece):
    return shift("group", 2, 1, 1)(piece)


def swap_core(piece):
    return shift("fsdp", 2, 1, 1)(piece)


def swap_half(piece):
    return shift("fsdp", 2, 2, 1)(piece)


def ring_gather(shard, ring):
    to_left, to_right = ring
    half = shard.shape[0] // 2
    right = to_left(shard)
    left = to_right(shard)
    return [shard, right, to_left(right[:half]), to_right(left[half:]), left]


def ring_sum(left_first, right_first, held_left, held_right, ring, beside=None):
    to_left, to_right = ring
    half = held_left.shape[0]
    from_right = to_left(left_first)
    from_left = to_right(right_first)
    if beside is not None:
        from_right, from_left, beside = lax.optimization_barrier((from_right, from_left, beside))
    from_right_last = to_left((held_left + from_right[:half].astype(F32)).astype(BF16))
    from_left_last = to_right((held_right + from_left[:half].astype(F32)).astype(BF16))
    sums = (from_left, from_right, from_right_last, from_left_last)
    return sums if beside is None else (sums, beside)


def ring_total(own, from_left, from_right, from_right_last, from_left_last):
    half = own.shape[0] // 2
    first = own[:half] + from_left[half:].astype(F32) + from_right_last.astype(F32)
    second = own[half:] + from_right[half:].astype(F32) + from_left_last.astype(F32)
    return jnp.concatenate([first, second])


def ordered(flag, own, other):
    first = jnp.where(flag == 0, own, other)
    second = jnp.where(flag == 0, other, own)
    return first, second


def core_rows(shards, core):
    keep, send = [], []
    for shard in shards:
        width = shard.shape[1] // 2
        low, high = shard[:, :width], shard[:, width:]
        keep.append(jnp.where(core == 0, low, high))
        send.append(jnp.where(core == 0, high, low))
    own = jnp.concatenate(keep, axis=1)
    other = swap_core(jnp.concatenate(send, axis=1))
    return jnp.concatenate(ordered(core, own, other))


def normalize_kernel(place_ref, values_ref, gain_ref, out_ref):
    blocks = 4
    width = values_ref.shape[1] // blocks
    values = values_ref[...].astype(F32)
    inverse_rms = lax.rsqrt(jnp.mean(values * values, axis=-1, keepdims=True) + EPSILON)
    for block in range(blocks):
        source = pl.multiple_of(lax.rem(place_ref[0] + block, blocks) * width, 128)
        part = values_ref[:, pl.ds(source, width)].astype(F32)
        out_ref[:, block * width : (block + 1) * width] = (
            part * inverse_rms * gain_ref[:, pl.ds(source, width)]
        ).astype(BF16)


def normalize_turned(values, gain_vector, places):
    return pl.pallas_call(
        normalize_kernel,
        out_shape=like(values.shape, BF16),
        in_specs=[SMEM, VMEM, VMEM],
        out_specs=VMEM,
        compiler_params=memory(16),
    )(places, values, gain_vector[None])


def unit_rows(values, scale):
    mean = jnp.mean(values * values, axis=-1, keepdims=True)
    return values * lax.rsqrt(mean + EPSILON) * scale


def dot(left, right, left_dim=1, right_dim=0):
    return lax.dot_general(
        left, right, (((left_dim,), (right_dim,)), ((), ())), preferred_element_type=F32
    )


def loop(count, body):
    lax.fori_loop(0, count, lambda index, carry: (body(index), carry)[1], 0)


def mix_scratch(tokens, width):
    return [
        pltpu.VMEM((tokens, width), BF16),
        pltpu.VMEM((width, tokens), BF16),
        pltpu.VMEM((tokens, width), BF16),
    ]


def mix_head(query, key, value, scratch, store):
    tokens, width = query.shape
    unit_query, turned_key, rounded = scratch
    unit_query[...] = unit_rows(query, LOG2_E * width**-0.5).astype(BF16)
    turned_key[...] = unit_rows(key, 1.0).T.astype(BF16)
    rounded[...] = value.astype(BF16)
    span = tokens // 3

    for first in range(0, tokens, span):
        weights = jnp.exp2(dot(unit_query[first : first + span, :], turned_key[...]))
        totals = jnp.sum(weights, axis=-1, keepdims=True)
        store(first, (dot(weights.astype(BF16), rounded[...]) / totals).astype(BF16))


def gather_parts(parts, target, sems):
    copies = []
    row = 0
    for index, part in enumerate(parts):
        rows = part.shape[0]
        copies.append(
            pltpu.make_async_copy(part, target.at[pl.ds(row, rows)], sems.at[index])
        )
        row += rows
    for copy in copies:
        copy.start()
    return copies


def head_kernel(count, *refs):
    parts, refs = refs[:count], refs[count:]
    buffer, projected, mixed, full, weight, query, key, value, sems, weight_sem = refs
    width = mixed.shape[1]
    copies = [
        pltpu.make_async_copy(buffer.at[:, pl.ds(0, 3 * width)], weight, weight_sem)
    ]
    copies[0].start()
    copies += gather_parts(parts, full, sems)
    for copy in copies:
        copy.wait()
    projected[...] = dot(full[...], weight[...])

    def store(first, rows):
        mixed[first : first + rows.shape[0], :] = rows

    mix_head(
        projected[:, :width],
        projected[:, width : 2 * width],
        projected[:, 2 * width :],
        (query, key, value),
        store,
    )


def generator_head(parts, buffer, keep):
    tokens = sum(part.shape[0] for part in parts)
    depth, width = buffer.shape[0], buffer.shape[1] // 4
    outs = [like((tokens, 3 * width), F32), like((tokens, width), BF16)]
    scratch = [pltpu.VMEM((depth, 3 * width), BF16)] + mix_scratch(tokens, width)
    scratch += [pltpu.SemaphoreType.DMA((len(parts),)), pltpu.SemaphoreType.DMA(())]
    if keep:
        outs.append(like((tokens, depth), BF16))
    else:
        scratch.insert(0, pltpu.VMEM((tokens, depth), BF16))
    return pl.pallas_call(
        functools.partial(head_kernel, len(parts)),
        out_shape=outs,
        in_specs=[ANY] * (len(parts) + 1),
        out_specs=[VMEM] * len(outs),
        scratch_shapes=scratch,
        compiler_params=memory(48),
    )(*parts, buffer)


def columns_kernel(places, buffer, out, sems):
    rows = out.shape[0] // 4
    first = buffer.shape[1] - out.shape[1]
    copies = []
    for block in range(4):
        place = pl.multiple_of(lax.rem(places[0] + block, 4) * rows, rows)
        copies.append(
            pltpu.make_async_copy(
                buffer.at[pl.ds(block * rows, rows), pl.ds(first, out.shape[1])],
                out.at[pl.ds(place, rows)],
                sems.at[block],
            )
        )
    for copy in copies:
        copy.start()
    for copy in copies:
        copy.wait()


def out_columns_in_order(places, buffer, width):
    return pl.pallas_call(
        columns_kernel,
        out_shape=like((buffer.shape[0], width), BF16),
        in_specs=[SMEM, ANY],
        out_specs=VMEM,
        scratch_shapes=[pltpu.SemaphoreType.DMA((4,))],
        compiler_params=memory(16),
    )(places, buffer)


def update_kernel(
    places, a_own, b_own, a_other, b_other, own_buffer, own_heads, other_buffer, other_heads,
    own, left, right, held_left, held_right, matrix, sems
):
    width = a_own.shape[1]
    size = own.shape[1] // 4
    copies = []
    for side, (buffer, heads) in enumerate(
        ((own_buffer, own_heads), (other_buffer, other_heads))
    ):
        for block in range(4):
            first = pl.multiple_of((2 * block + places[1]) * size, size)
            rows = pl.ds(block * size, size)
            for index, source in enumerate(
                (buffer.at[pl.ds(first, size), pl.ds(3 * width, width)], heads.at[rows])
            ):
                target = matrix.at[rows, pl.ds((2 * side + index) * width, width)]
                copies.append(
                    pltpu.make_async_copy(source, target, sems.at[side, 2 * block + index])
                )
    for copy in copies:
        copy.start()
    for copy in copies:
        copy.wait()
    mixed = jnp.concatenate([a_own[...], b_own[...], a_other[...], b_other[...]], axis=1)
    rows = own.shape[0]
    half = rows // 2

    def term(first, count):
        return dot(mixed[first : first + count], matrix[...], 1, 1)

    two = term(2 * rows, rows)
    left[:half, :] = two[:half].astype(BF16)
    right[:half, :] = two[half:].astype(BF16)
    three = term(3 * rows, rows)
    held_left[...] = three[:half]
    left[half:, :] = three[half:].astype(BF16)
    one = term(rows, rows)
    right[half:, :] = one[:half].astype(BF16)
    held_right[...] = one[half:]
    own[...] = term(0, rows)


def update_terms(places, mixed, weights, rows):
    width = weights[0].shape[0] // 2
    return pl.pallas_call(
        update_kernel,
        out_shape=[
            like((rows, width), F32),
            like((rows, width), BF16),
            like((rows, width), BF16),
            like((rows // 2, width), F32),
            like((rows // 2, width), F32),
        ],
        in_specs=[SMEM] + [VMEM] * 4 + [ANY] * 4,
        out_specs=[VMEM] * 5,
        scratch_shapes=[
            pltpu.VMEM((width, weights[0].shape[1]), BF16),
            pltpu.SemaphoreType.DMA((2, 8)),
        ],
        compiler_params=memory(24),
    )(places, *mixed, *weights)


def noisy_rows(level, generated, noise):
    return ((1.0 - level) * generated.astype(F32) + level * noise.astype(F32)).astype(BF16)


def generate_kernel(
    places, level, latent, noise, own, from_left, from_right, right_last, left_last, generated, noisy
):
    half = own.shape[0] // 2
    width = own.shape[1] // 4
    for block in range(4):
        columns = slice(block * width, (block + 1) * width)
        source = (lax.rem(places[0] + block, 4) * 2 + places[1]) * width
        source = pl.ds(pl.multiple_of(source, 128), width)
        for rows, near, last in (
            (slice(0, half), from_left, right_last),
            (slice(half, 2 * half), from_right, left_last),
        ):
            update = own[rows, columns] + near[half:, columns].astype(F32)
            update = update + last[:, columns].astype(F32)
            made = (latent[rows, source].astype(F32) + update).astype(BF16)
            generated[rows, columns] = made
            noisy[rows, columns] = noisy_rows(level[0], made, noise[rows, source])


def generate_half(places, level, latent, noise, terms):
    shape = terms[0].shape
    return pl.pallas_call(
        generate_kernel,
        out_shape=[like(shape, BF16), like(shape, BF16)],
        in_specs=[SMEM] * 2 + [VMEM] * 7,
        out_specs=[VMEM] * 2,
        compiler_params=memory(24),
    )(places, level, latent, noise, *terms)


def join_kernel(places, level, own, other, noise, generated, noisy):
    width = own.shape[1] // 4
    for block in range(4):
        columns = slice(block * width, (block + 1) * width)
        pair = lax.rem(places[0] + block, 4) * 2
        here = pl.ds(pl.multiple_of((pair + places[1]) * width, 128), width)
        there = pl.ds(pl.multiple_of((pair + 1 - places[1]) * width, 128), width)
        generated[:, here] = own[:, columns]
        made = other[:, columns]
        generated[:, there] = made
        noisy[:, columns] = noisy_rows(level[0], made, noise[:, there])


def join_halves(places, level, own, other, noise):
    return pl.pallas_call(
        join_kernel,
        out_shape=[like(noise.shape, BF16), like(own.shape, BF16)],
        in_specs=[SMEM] * 2 + [VMEM] * 3,
        out_specs=[VMEM] * 2,
        compiler_params=memory(24),
    )(places, level, own, other, noise)


def half_weight_copies(places, matrix, weight, sems, side, head):
    copies = []
    size = matrix.shape[2] // 8
    for block in range(4):
        first = (lax.rem(places[0] + block, 4) * 2 + side) * size
        rows = pl.ds(pl.multiple_of(first, size), size)
        copies.append(
            pltpu.make_async_copy(
                matrix.at[:, head, rows],
                weight.at[head, :, pl.ds(block * size, size)],
                sems.at[head, block],
            )
        )
    return copies


def head_weight(weight, head):
    return jnp.concatenate([weight[head, kind] for kind in range(weight.shape[1])], axis=1)


def scale_rows(places, side, full, gain, squares):
    size = gain.shape[1] // 8
    span = 96

    def scale(index):
        rows = pl.ds(pl.multiple_of(index * span, span), span)
        values = full[rows, :].astype(F32)
        sums = jnp.sum(values * values, axis=-1, keepdims=True)
        squares[rows, :] = jnp.broadcast_to(sums, (span, squares.shape[1]))
        for block in range(4):
            first = (lax.rem(places[0] + block, 4) * 2 + side) * size
            part = gain[:, pl.ds(pl.multiple_of(first, 128), size)]
            columns = slice(block * size, (block + 1) * size)
            full[rows, columns] = (values[:, columns] * part).astype(BF16)

    loop(full.shape[0] // span, scale)


def score_kernel(places, *refs):
    own_parts, parts, refs = refs[:5], refs[5:10], refs[10:]
    back_source, matrix, gain = refs[:3]
    outs = [refs[3:8], refs[8:13]]
    (
        own_full, full, own_weight, weight, back, mixed, own_squares, squares, inverse_rms,
        query, key, value, own_part_sems, part_sems, own_sems, sems, back_sem,
    ) = refs[13:]
    heads = sems.shape[0]
    width = weight.shape[1] * weight.shape[3]
    head_width = width // 3
    tokens = full.shape[0]
    step = tokens // 4
    half = tokens // 2

    def head_copies(head):
        return half_weight_copies(
            places, matrix, own_weight, own_sems, places[1], head
        ) + half_weight_copies(places, matrix, weight, sems, 1 - places[1], head)

    own_copies = gather_parts(own_parts, own_full, own_part_sems)
    copies = gather_parts(parts, full, part_sems)
    for head in range(heads):
        for copy in head_copies(head):
            copy.start()
    back_copy = pltpu.make_async_copy(back_source, back, back_sem)
    back_copy.start()
    for copy in own_copies:
        copy.wait()
    scale_rows(places, places[1], own_full, gain, own_squares)
    for copy in copies:
        copy.wait()
    scale_rows(places, 1 - places[1], full, gain, squares)
    mean = (own_squares[...] + squares[...]) / (2 * full.shape[1])
    inverse_rms[...] = lax.rsqrt(mean + EPSILON)

    def one_head(head):
        for copy in head_copies(head):
            copy.wait()
        projected = dot(own_full[...], head_weight(own_weight, head))
        projected = projected + dot(full[...], head_weight(weight, head))
        lanes = pl.ds(pl.multiple_of(head * head_width, 128), head_width)

        def store(first, rows):
            mixed[first : first + rows.shape[0], lanes] = rows

        mix_head(
            *[
                projected[:, kind * head_width : (kind + 1) * head_width] * inverse_rms[...]
                for kind in range(3)
            ],
            (query, key, value),
            store,
        )

    loop(heads, one_head)
    back_copy.wait()

    def back_part(block, flip):
        pair = (block * 2 + flip) * 2
        return jnp.concatenate([back[pair + places[2]], back[pair + 1 - places[2]]])

    for flip, (own, left, right, held_left, held_right) in zip((1, 0), outs):

        def term(block):
            start = block * step
            rows = mixed[...]
            if block:
                rows = jnp.concatenate([mixed[start:, :], mixed[:start, :]])
            return dot(rows, back_part(block, flip), 1, 1)

        two = term(2)
        left[:half, :] = two[:half].astype(BF16)
        right[:half, :] = two[half:].astype(BF16)
        three = term(3)
        held_left[...] = three[:half]
        left[half:, :] = three[half:].astype(BF16)
        one = term(1)
        right[half:, :] = one[:half].astype(BF16)
        held_right[...] = one[half:]
        own[...] = term(0)


def score_terms(places, own_parts, parts, matrix, back, gain):
    tokens = sum(part.shape[0] for part in parts)
    kinds, heads, _, head_width = matrix.shape
    depth = parts[0].shape[1]
    columns = 2 * back.shape[1]
    one = [
        like((tokens, columns), F32),
        like((tokens, columns), BF16),
        like((tokens, columns), BF16),
        like((tokens // 2, columns), F32),
        like((tokens // 2, columns), F32),
    ]
    outs = pl.pallas_call(
        score_kernel,
        out_shape=one + one,
        in_specs=[SMEM] + [ANY] * 12 + [VMEM],
        out_specs=[VMEM] * 10,
        scratch_shapes=[
            pltpu.VMEM((tokens, depth), BF16),
            pltpu.VMEM((tokens, depth), BF16),
            pltpu.VMEM((heads, kinds, depth, head_width), BF16),
            pltpu.VMEM((heads, kinds, depth, head_width), BF16),
            pltpu.VMEM(back.shape, BF16),
            pltpu.VMEM((tokens, heads * head_width), BF16),
            pltpu.VMEM((tokens, 128), F32),
            pltpu.VMEM((tokens, 128), F32),
            pltpu.VMEM((tokens, 128), F32),
            *mix_scratch(tokens, head_width),
            pltpu.SemaphoreType.DMA((5,)),
            pltpu.SemaphoreType.DMA((5,)),
            pltpu.SemaphoreType.DMA((heads, 4)),
            pltpu.SemaphoreType.DMA((heads, 4)),
            pltpu.SemaphoreType.DMA(()),
        ],
        compiler_params=memory(36),
    )(places, *own_parts, *parts, back, matrix, gain)
    return outs[:5], outs[5:]


def unit_reverse(values, gradient, scale):
    width = values.shape[-1]
    inverse = lax.rsqrt(jnp.mean(values * values, axis=-1, keepdims=True) + EPSILON)
    along = jnp.sum(gradient * values, axis=-1, keepdims=True) / width
    return scale * inverse * (gradient - values * (along * inverse * inverse))


def reverse_kernel(projected, gradient, out, key_total, value_total):
    tokens, width = gradient.shape
    query, key = projected[:, :width], projected[:, width : 2 * width]
    scale = width**-0.5
    unit_query = unit_rows(query, LOG2_E * scale).astype(BF16)
    unit_key = unit_rows(key, 1.0).astype(BF16)
    value = projected[:, 2 * width :]
    turned_key = unit_rows(key, 1.0).T.astype(BF16)
    turned_value = value.T.astype(BF16)
    value = value.astype(BF16)
    span = tokens // 3
    for first in range(0, tokens, span):
        rows = slice(first, first + span)
        weights = jnp.exp2(dot(unit_query[rows], turned_key))
        totals = jnp.sum(weights, axis=-1, keepdims=True)
        rounded = weights.astype(BF16)
        raw = dot(rounded, value)
        given = gradient[rows, :].astype(F32)
        draw = (given / totals).astype(BF16)
        dtotals = -jnp.sum(given * raw, axis=-1, keepdims=True) / (totals * totals)
        dweights = dot(draw, turned_value).astype(BF16).astype(F32) + dtotals
        dscores = (dweights * weights).astype(BF16)
        dquery = dot(dscores, unit_key).astype(BF16).astype(F32)
        out[rows, :width] = unit_reverse(query[rows], dquery, scale).astype(BF16)
        key_term = dot(dscores, unit_query[rows], 0, 0)
        value_term = dot(rounded, draw, 0, 0)
        if first == 0:
            key_total[...] = key_term
            value_total[...] = value_term
        else:
            key_total[...] += key_term
            value_total[...] += value_term
    dkey = (LN_2 * key_total[...]).astype(BF16).astype(F32)
    out[:, width : 2 * width] = unit_reverse(key, dkey, 1.0).astype(BF16)
    out[:, 2 * width :] = value_total[...].astype(BF16)


def reverse_head(projected, gradient):
    tokens, width = gradient.shape
    return pl.pallas_call(
        reverse_kernel,
        out_shape=like(projected.shape, BF16),
        in_specs=[VMEM] * 2,
        out_specs=VMEM,
        scratch_shapes=[pltpu.VMEM((tokens, width), F32), pltpu.VMEM((tokens, width), F32)],
        compiler_params=memory(24),
    )(projected, gradient)


def local(latent_in, noise, timestep, gen_gain, gen_qkv, gen_out, score_gain, score_qkv, score_out):
    place = lax.axis_index("fsdp")
    core, x_half, y_place = place % 2, (place // 2) % 2, place // 4
    group = lax.axis_index("group")
    fsdp_size = lax.axis_size("fsdp")
    seq_size = lax.axis_size("seq")
    group_size = lax.axis_size("group")
    head_width = gen_qkv.shape[-1]
    gen_heads = gen_qkv.shape[1]
    model_width = latent_in.shape[2]
    local_rows = latent_in.shape[1]
    places = jnp.stack([y_place, group, core]).astype(jnp.int32)

    fraction = (timestep[0].astype(F32) + 1.0) / STEPS
    noise_level = SHIFT_FACTOR * fraction / (1.0 + (SHIFT_FACTOR - 1.0) * fraction)
    level = noise_level.reshape(1)

    left_z, right_z = seq_ring()
    left_y, right_y = y_ring()
    normed = normalize_turned(latent_in[0], gen_gain, places)
    pair = core_rows(
        [gen_qkv.reshape(gen_qkv.shape[0], -1), gen_out.reshape(gen_out.shape[0], -1)], core
    )
    normed, pair = lax.optimization_barrier((normed, pair))
    right_shard, left_shard = left_z(normed), right_z(normed)
    block = jnp.concatenate(ordered(x_half, pair, swap_half(pair)))
    block, score_qkv = lax.optimization_barrier((block, score_qkv))
    score_matrix = jnp.transpose(score_qkv[:, 0], (2, 1, 0, 3))
    right_block, left_block = left_y(block), right_y(block)
    right_shard, left_shard, score_matrix = lax.optimization_barrier(
        (right_shard, left_shard, score_matrix)
    )

    half = local_rows // 2
    rows = block.shape[0] // 2
    far_first, far_second, right_far, left_far, right_block, left_block = lax.optimization_barrier(
        (
            left_z(right_shard[:half]),
            right_z(left_shard[half:]),
            left_y(right_block[:rows]),
            right_y(left_block[rows:]),
            right_block,
            left_block,
        )
    )
    own_buffer = jnp.concatenate([block, right_block, right_far, left_far, left_block])
    other_buffer = swap_core(own_buffer)

    out_columns = own_buffer[:, 3 * head_width :]
    out_halves = out_columns.reshape(4, 2, -1, head_width)
    own_heads = swap_group(jnp.where(group == 0, out_halves[:, 1], out_halves[:, 0]))
    own_heads = own_heads.reshape(-1, head_width)

    moves = []
    for g in range(group_size):
        for f in range(fsdp_size):
            for s in range(seq_size):
                source = ((g ^ ((f // 2) % 2)) * fsdp_size + f) * seq_size + (s + f // 4) % seq_size
                moves.append((source, (g * fsdp_size + f) * seq_size + s))
    normed_parts = [normed, right_shard, far_first, far_second, left_shard]
    own_projected, own_mixed = generator_head(normed_parts, own_buffer, False)
    own_heads, own_mixed = lax.optimization_barrier((own_heads, own_mixed))
    other_heads = swap_core(own_heads)
    own_partner = swap_group(own_mixed)
    other_projected, other_mixed, normed_full = generator_head(
        normed_parts, other_buffer, True
    )
    other_mixed, buffer = lax.optimization_barrier((other_mixed, own_buffer))
    other_partner = swap_group(other_mixed)
    head_columns = lax.ppermute(
        out_columns_in_order(places, buffer, head_width), ("group", "fsdp", "seq"), moves
    )

    terms = update_terms(
        places,
        [own_mixed, own_partner, other_mixed, other_partner],
        [own_buffer, own_heads, other_buffer, other_heads],
        local_rows,
    )
    sums, head_columns = ring_sum(*terms[1:], seq_ring(), head_columns)
    polarity = (2 * group - 1).astype(F32)
    back_block = dot(head_columns, score_out[:, 0].reshape(model_width, -1), 0, 0)
    back_block = (polarity * back_block).astype(BF16)
    back_blocks = lax.all_gather(back_block, "fsdp", axis=0)
    *sums, _ = lax.optimization_barrier((*sums, back_block))
    own_made, own_noisy = generate_half(
        places, level, latent_in[0], noise[0], [terms[0], *sums]
    )
    other_made = swap_group(own_made)
    own_parts = ring_gather(own_noisy, seq_ring())
    generated, other_noisy = join_halves(places, level, own_made, other_made, noise[0])
    other_parts = ring_gather(other_noisy, seq_ring())

    flipped, straight = score_terms(
        places, own_parts, other_parts, score_matrix, back_blocks, score_gain
    )

    flipped_sum = ring_total(flipped[0], *ring_sum(*flipped[1:], seq_ring()))
    flipped_sum = swap_group(flipped_sum.astype(BF16))
    dmixed = ring_total(straight[0], *ring_sum(*straight[1:], seq_ring()))
    dmixed = (dmixed + flipped_sum.astype(F32)) * (-noise_level / float(fsdp_size))
    dmixed = dmixed.astype(BF16)

    dother = reverse_head(other_projected, dmixed[:, head_width:])
    sent = dot(normed_full, dother, 0, 0).astype(BF16)
    got = swap_core(sent)
    down = reverse_head(own_projected, dmixed[:, :head_width])
    pair = (dot(normed_full, down, 0, 0) + got.astype(F32)).reshape(4, model_width // 4, -1)
    rows = pair.shape[1] // 2
    summed = ring_total(
        pair[0],
        *ring_sum(
            jnp.concatenate([pair[2, :rows], pair[3, rows:]]).astype(BF16),
            jnp.concatenate([pair[2, rows:], pair[1, :rows]]).astype(BF16),
            pair[3, :rows],
            pair[1, rows:],
            y_ring(),
        ),
    )
    rows = rows // 2

    def rows_of(x, c):
        return lax.dynamic_slice_in_dim(summed, (2 * x + c) * rows, rows)

    over_x = swap_half(rows_of(1 - x_half, core).astype(BF16))
    over_core = swap_core(rows_of(x_half, 1 - core).astype(BF16))
    over_both = lax.ppermute(
        rows_of(1 - x_half, 1 - core).astype(BF16), "fsdp", [(i, i ^ 3) for i in range(fsdp_size)]
    )
    own_head = rows_of(x_half, core) + over_x.astype(F32)
    other_head = over_core.astype(F32) + over_both.astype(F32)
    gen_grad = jnp.concatenate(ordered(core, own_head, other_head), axis=1)
    return (generated[None], gen_grad.reshape(-1, gen_heads, 3, head_width))


def solution(mesh):
    in_specs = (
        P("fsdp", "seq", None),
        P("fsdp", "seq", None),
        P("fsdp"),
        P(),
        P("fsdp", ("group", "seq"), None, None),
        P("fsdp", ("group", "seq"), None),
        P("group", None),
        P(None, "group", "seq", None, None),
        P(None, "group", "seq", None),
    )
    out_specs = (P("fsdp", "seq", None), P("fsdp", ("group", "seq"), None, None))
    return jax.shard_map(local, mesh=mesh, in_specs=in_specs, out_specs=out_specs, check_vma=False)
```
